32 devices in a mesh: groups: 2 (over y), ex: 4 (over z), ckpt: 2 (over x), dim: 2 (over core).
Axes of the slice: x: 2, y: 2, z: 4, core: 2. Of those that a mesh axis runs over, the one named last changes fastest.
Arguments:
- train_features: bfloat16 [8, 8192, 2048], P('ckpt', ('groups', 'ex'), 'dim'), parts along dimension 1, may hold values from -6 to 6
- query_features: bfloat16 [8, 2048, 2048], P('ckpt', ('groups', 'ex'), 'dim'), parts along dimension 1, may hold values from -0.5 to 0.5
- residual_weights: float32 [8, 8192], P('ckpt', ('groups', 'ex')), parts along dimension 1, may hold values from 0.05 to 1
Outputs:
- scores: float32 [1024, 8192], P(('ckpt', 'dim'), ('groups', 'ex')), parts along dimension 1
The draws below stay inside these ranges and needn't reach their ends.
There are 2 independent parts, one for each index of `groups`. The reference program is written for one: setup_inputs(seed, part) draws one part's arguments, and reference() takes and returns one part's arrays. A program takes and returns all parts, laid end to end along the dimension named above; each array names one. Nothing has to cross between parts.
All inputs are finite; a program needn't handle non-finite values.
Results may differ from the reference program's by a relative error of at most 0.0003.
Values may be sent and summed in bfloat16 or wider, within the bound.
No kernel may reach another device: no remote copies, remote signals or barrier semaphores. Data moves between devices by JAX's collectives and lax.ppermute only.
A program may use at most 64 MiB of HBM per device.

```python
import math
import jax
import jax.numpy as jnp
from jax import lax

PROJ = 2048
QUERIES = 1024
EXAMPLES = 4096
CKPTS = 8


def steps_of(stream_key, dims, split, smallest, high):
    def one(position, shards_of):
        draws = jax.random.uniform(jax.random.fold_in(jax.random.fold_in(stream_key, 6), position), (shards_of,), jnp.float32, smallest / len(split), high / len(split))
        return jnp.repeat(jnp.exp(draws), dims[position] // shards_of).reshape((-1,) + (1,) * (len(dims) - position - 1))

    loudness = one(*split[0])
    for cut in split[1:]:
        loudness = loudness * one(*cut)
    return loudness


def noise(key, dims, spread, most, cuts=(), dtype=jnp.bfloat16):
    level = steps_of(key, dims, cuts, -0.22, 0.18) if cuts else 1.0
    drawn = jax.random.normal(key, dims, jnp.float32) * spread * level
    return jnp.minimum(jnp.maximum(drawn, -most), most).astype(dtype)


def setup_inputs(seed: int = 0, part: int = 0) -> dict:
    key_of = jax.random.split(jax.random.key(seed), 4)
    own_keys = jax.random.split(jax.random.fold_in(key_of[3], part), 4)
    train_features = noise(own_keys[0], (CKPTS, EXAMPLES, PROJ), 1.0, 6.0, ((0, 2), (1, 4), (2, 2)))
    query_features = noise(own_keys[1], (CKPTS, QUERIES, PROJ), (PROJ // 16) ** -0.5, 0.5, ((0, 2), (1, 4), (2, 2)))
    residual_weights = jnp.clip(jnp.exp(math.log(1.0) - 2.9957323 * jax.random.uniform(own_keys[2], (CKPTS, EXAMPLES), jnp.float32) ** steps_of(own_keys[2], (CKPTS, EXAMPLES), ((0, 2), (1, 4)), -0.2, 0.2)), 0.05, 1.0)
    return {"train_features": train_features, "query_features": query_features, "residual_weights": residual_weights}


def reference(train_features, query_features, residual_weights):
    def one_checkpoint(total, inputs):
        train_one, query_one, weight_one = inputs
        dots = jnp.dot(query_one.astype(jnp.float32), train_one.astype(jnp.float32).T)
        return total + dots * weight_one[None, :], None

    start = jnp.zeros((QUERIES, EXAMPLES), jnp.float32)
    total, unused = lax.scan(one_checkpoint, start, (train_features, query_features, residual_weights))
    return total * (1.0 / CKPTS)
```

```python
import jax
import jax.numpy as jnp
from jax import lax
from jax.sharding import PartitionSpec as P

PLACE = ("ex", "ckpt", "dim")


def block_scores(piece, train_features, residual_weights, scale):
    total = None
    for check in range(piece.shape[0]):
        dots = lax.dot_general(
            piece[check],
            train_features[check],
            (((1,), (1,)), ((), ())),
            preferred_element_type=jnp.float32,
        )
        term = dots * residual_weights[check][None, :]
        total = term if total is None else total + term
    return total * scale


def summed_at_owner(partial, owners):
    ckpts, dims = lax.axis_size("ckpt"), lax.axis_size("dim")

    def index(z, x, c):
        return (z * ckpts + x) * dims + c

    total = partial
    for away in range(1, dims):
        pairs = []
        for z, owner in enumerate(owners):
            if owner is not None:
                for x in range(ckpts):
                    pairs.append((index(z, x, (owner[1] + away) % dims), index(z, x, owner[1])))
        total = total + lax.ppermute(partial, PLACE, pairs)
    whole = total
    for away in range(1, ckpts):
        pairs = []
        for z, owner in enumerate(owners):
            if owner is not None:
                pairs.append((index(z, (owner[0] + away) % ckpts, owner[1]), index(z, *owner)))
        whole = whole + lax.ppermute(total, PLACE, pairs)
    return whole


def local(train_features, query_features, residual_weights):
    planes = lax.axis_size("ex")
    ckpts, dims = lax.axis_size("ckpt"), lax.axis_size("dim")
    z = lax.axis_index("ex")
    place = lax.axis_index("ckpt") * dims + lax.axis_index("dim")
    scale = 1.0 / (train_features.shape[0] * ckpts)
    rows = query_features.shape[1]
    kept = rows * planes // (ckpts * dims)
    ratio = kept // rows
    assert ratio * rows == kept
    pieces = 4 if rows % 64 == 0 else 1

    results = [[None] * pieces for unused in range(ratio)]

    def finish(found, blocks, start):
        owners = []
        for block in blocks:
            if block is None:
                owners.append(None)
            else:
                owner = block // ratio
                owners.append((owner // dims, owner % dims))
        whole = summed_at_owner(found, owners)
        numbers = jnp.array([-1 if block is None else block for block in blocks], jnp.int32)
        number = numbers[z]
        step = rows // pieces
        for j in range(ratio):
            mine = number == place * ratio + j
            for k in range(found.shape[0] // step):
                part = whole[k * step:(k + 1) * step]
                at = start // step + k
                old = results[j][at]
                results[j][at] = part if old is None else jnp.where(mine, part, old)

    def scores(piece):
        return block_scores(piece, train_features, residual_weights, scale)

    rights, lefts = [query_features], [query_features]
    for step in range(1, planes):
        right = [(s, s + 1) for s in range(step - 1, planes - 1)]
        left = [(s, s - 1) for s in range(1, planes - step + 1)]
        cut = pieces if step == planes - 1 else 1
        size = rows // cut
        new_rights, new_lefts = [], []
        for k in range(cut):
            from_left = rights[0] if cut == 1 else rights[0][:, k * size:(k + 1) * size]
            from_right = lefts[0] if cut == 1 else lefts[0][:, k * size:(k + 1) * size]
            if 2 * step > planes + 1:
                sent = jnp.where(z >= step - 1, from_left, from_right)
                got = lax.ppermute(sent, "ex", right + left)
                new_rights.append(got)
                new_lefts.append(got)
            else:
                new_rights.append(lax.ppermute(from_left, "ex", right))
                new_lefts.append(lax.ppermute(from_right, "ex", left))
        if step == 1:
            finish(scores(query_features), list(range(planes)), 0)
        for k in range(cut):
            blocks_right = [s - step if s >= step else None for s in range(planes)]
            blocks_left = [s + step if s + step < planes else None for s in range(planes)]
            if 2 * step >= planes:
                got = jnp.where(z >= step, new_rights[k], new_lefts[k])
                both = [a if a is not None else b for a, b in zip(blocks_right, blocks_left)]
                finish(scores(got), both, k * size)
            else:
                finish(scores(new_rights[k]), blocks_right, k * size)
                finish(scores(new_lefts[k]), blocks_left, k * size)
        rights, lefts = new_rights, new_lefts
    return jnp.concatenate([part for block in results for part in block], axis=0)


def solution(mesh):
    in_specs = (
        P("ckpt", ("groups", "ex"), "dim"),
        P("ckpt", ("groups", "ex"), "dim"),
        P("ckpt", ("groups", "ex")),
    )
    out_specs = P(("ckpt", "dim"), ("groups", "ex"))
    return jax.shard_map(local, mesh=mesh, in_specs=in_specs, out_specs=out_specs, check_vma=False)
```

```python
import jax
import jax.numpy as jnp
from jax import lax
from jax.sharding import PartitionSpec as P

PLACE = ("ex", "ckpt", "dim")


def block_scores(piece, train_features, residual_weights, scale):
    total = None
    for check in range(piece.shape[0]):
        dots = lax.dot_general(
            piece[check],
            train_features[check],
            (((1,), (1,)), ((), ())),
            preferred_element_type=jnp.float32,
        )
        term = dots * residual_weights[check][None, :]
        total = term if total is None else total + term
    return total * scale


def summed_at_owner(partial, owners):
    ckpts, dims = lax.axis_size("ckpt"), lax.axis_size("dim")

    def index(z, x, c):
        return (z * ckpts + x) * dims + c

    total = partial
    for away in range(1, dims):
        pairs = []
        for z, owner in enumerate(owners):
            if owner is not None:
                for x in range(ckpts):
                    pairs.append((index(z, x, (owner[1] + away) % dims), index(z, x, owner[1])))
        total = total + lax.ppermute(partial, PLACE, pairs)
    whole = total
    for away in range(1, ckpts):
        pairs = []
        for z, owner in enumerate(owners):
            if owner is not None:
                pairs.append((index(z, (owner[0] + away) % ckpts, owner[1]), index(z, *owner)))
        whole = whole + lax.ppermute(total, PLACE, pairs)
    return whole


def local(train_features, query_features, residual_weights):
    planes = lax.axis_size("ex")
    ckpts, dims = lax.axis_size("ckpt"), lax.axis_size("dim")
    z = lax.axis_index("ex")
    place = lax.axis_index("ckpt") * dims + lax.axis_index("dim")
    scale = 1.0 / (train_features.shape[0] * ckpts)
    rows = query_features.shape[1]
    kept = rows * planes // (ckpts * dims)
    ratio = kept // rows
    assert ratio * rows == kept
    pieces = 4 if rows % 64 == 0 else 1

    results = [[None] * pieces for unused in range(ratio)]

    def finish(found, blocks, start):
        owners = []
        for block in blocks:
            if block is None:
                owners.append(None)
            else:
                owner = block // ratio
                owners.append((owner // dims, owner % dims))
        whole = summed_at_owner(found, owners)
        numbers = jnp.array([-1 if block is None else block for block in blocks], jnp.int32)
        number = numbers[z]
        step = rows // pieces
        for j in range(ratio):
            mine = number == place * ratio + j
            for k in range(found.shape[0] // step):
                part = whole[k * step:(k + 1) * step]
                at = start // step + k
                old = results[j][at]
                results[j][at] = part if old is None else jnp.where(mine, part, old)

    def scores(piece):
        return block_scores(piece, train_features, residual_weights, scale)

    right = [(s, (s + 1) % planes) for s in range(planes)]
    left = [(s, (s - 1) % planes) for s in range(planes)]
    from_left = from_right = query_features
    for step in range(1, planes // 2):
        from_left = lax.ppermute(from_left, "ex", right)
        from_right = lax.ppermute(from_right, "ex", left)
        if step == 1:
            finish(scores(query_features), list(range(planes)), 0)
        finish(scores(from_left), [(s - step) % planes for s in range(planes)], 0)
        finish(scores(from_right), [(s + step) % planes for s in range(planes)], 0)
    half = rows // 2
    top = lax.ppermute(from_left[:, :half], "ex", right)
    low = lax.ppermute(from_right[:, half:], "ex", left)
    across = [(s + planes // 2) % planes for s in range(planes)]
    finish(scores(top), across, 0)
    finish(scores(low), across, half)
    return jnp.concatenate([part for block in results for part in block], axis=0)


def solution(mesh):
    in_specs = (
        P("ckpt", ("groups", "ex"), "dim"),
        P("ckpt", ("groups", "ex"), "dim"),
        P("ckpt", ("groups", "ex")),
    )
    out_specs = P(("ckpt", "dim"), ("groups", "ex"))
    return jax.shard_map(local, mesh=mesh, in_specs=in_specs, out_specs=out_specs, check_vma=False)
```

```python
import jax
import jax.numpy as jnp
from jax import lax
from jax.sharding import PartitionSpec as P

PLACE = ("ex", "ckpt", "dim")
CHUNKS = 4


def after(value, *others):
    return lax.optimization_barrier((value,) + others)[0]


def weighted(checks, train, weights, scale):
    total = None
    for piece, examples, weight in zip(checks, train, weights):
        dots = lax.dot_general(
            piece,
            examples,
            (((1,), (1,)), ((), ())),
            preferred_element_type=jnp.float32,
        )
        term = dots * weight[None, :]
        total = term if total is None else total + term
    return total * scale


class Keepers:
    def __init__(self, rows):
        self.ckpts, self.dims = lax.axis_size("ckpt"), lax.axis_size("dim")
        self.planes = lax.axis_size("ex")
        self.z, self.x, self.c = [lax.axis_index(name) for name in PLACE]
        kept = rows * self.planes // (self.ckpts * self.dims)
        self.ratio = kept // rows
        assert self.ratio * rows == kept

    def index(self, z, x, c):
        return (z * self.ckpts + x) * self.dims + c

    def of(self, block):
        owner = block // self.ratio
        return owner // self.dims, owner % self.dims

    def mine(self, blocks, j=0):
        found = jnp.bool_(False)
        for z, block in enumerate(blocks):
            if block is not None and block % self.ratio == j:
                x, c = self.of(block)
                found = found | ((self.z == z) & (self.x == x) & (self.c == c))
        return found

    def sums(self, partial, blocks):
        total = partial
        for away in range(1, self.dims):
            pairs = []
            for z, block in enumerate(blocks):
                if block is not None:
                    c = self.of(block)[1]
                    for x in range(self.ckpts):
                        pairs.append((self.index(z, x, (c + away) % self.dims), self.index(z, x, c)))
            total = total + lax.ppermute(partial, PLACE, pairs)
        whole = total
        for away in range(1, self.ckpts):
            pairs = []
            for z, block in enumerate(blocks):
                if block is not None:
                    x, c = self.of(block)
                    pairs.append((self.index(z, (x + away) % self.ckpts, c), self.index(z, x, c)))
            whole = whole + lax.ppermute(total, PLACE, pairs)
        return whole

    def two_sums(self, one, one_blocks, two, two_blocks):
        keeps_one = jnp.bool_(False)
        swaps, crosses = [], []
        for z, blocks in enumerate(zip(one_blocks, two_blocks)):
            if blocks[0] is None:
                continue
            places = [self.of(block) for block in blocks]
            assert {places[0][1], places[1][1]} == {0, 1}
            keeps_one = keeps_one | ((self.z == z) & (self.c == places[0][1]))
            for at, c in places:
                for x in range(2):
                    swaps.append((self.index(z, x, 1 - c), self.index(z, x, c)))
                crosses.append((self.index(z, 1 - at, c), self.index(z, at, c)))
        got = lax.ppermute(jnp.where(keeps_one, two, one), PLACE, swaps)
        total = jnp.where(keeps_one, one, two) + got
        return total + lax.ppermute(total, PLACE, crosses)


def ring(train_features, query_features, residual_weights, keepers, scale):
    planes, ratio = keepers.planes, keepers.ratio
    rows = query_features.shape[1]
    half = rows // 2
    results = [[None, None] for unused in range(ratio)]

    def finish(piece, blocks, start):
        found = weighted(list(piece), train_features, residual_weights, scale)
        whole = keepers.sums(found, blocks)
        for j in range(ratio):
            mine = keepers.mine(blocks, j)
            for k in range(found.shape[0] // half):
                part = whole[k * half:(k + 1) * half]
                at = start // half + k
                old = results[j][at]
                results[j][at] = part if old is None else jnp.where(mine, part, old)

    right = [(s, (s + 1) % planes) for s in range(planes)]
    left = [(s, (s - 1) % planes) for s in range(planes)]
    from_left = from_right = query_features
    finish(query_features, list(range(planes)), 0)
    for step in range(1, planes // 2):
        from_left = lax.ppermute(from_left, "ex", right)
        from_right = lax.ppermute(from_right, "ex", left)
        finish(from_left, [(s - step) % planes for s in range(planes)], 0)
        finish(from_right, [(s + step) % planes for s in range(planes)], 0)
    across = [(s + planes // 2) % planes for s in range(planes)]
    finish(lax.ppermute(from_left[:, :half], "ex", right), across, 0)
    finish(lax.ppermute(from_right[:, half:], "ex", left), across, half)
    return jnp.concatenate([part for block in results for part in block], axis=0)


def line(train_features, query_features, residual_weights, keepers, scale):
    z = keepers.z
    rows = query_features.shape[1]
    most = train_features.shape[0] - 1
    examples = train_features.shape[1]
    half, cut = examples // 2, rows // CHUNKS
    ends = (z == 0) | (z == 3)

    def inward(value):
        return lax.ppermute(value, "ex", [(0, 1), (3, 2)])

    def between(value):
        return lax.ppermute(value, "ex", [(1, 2), (2, 1)])

    def outward(value):
        return lax.ppermute(value, "ex", [(1, 0), (2, 3)])

    own_many, own_one = query_features[:most], query_features[most]
    train_one = train_features[most]

    out_own = outward(own_many)
    in_one = inward(own_one)
    mid_one = between(own_one)
    in_weight = inward(residual_weights[most:])[0]
    in_train = [inward(after(train_one[:half], in_weight))]
    mid_many = [between(own_many[0])]
    out_many = [outward(mid_many[0])]
    mid_many.append(between(after(own_many[1], mid_one)))
    out_many.append(outward(mid_many[1]))
    mid_many.append(between(after(own_many[2], mid_many[0])))
    out_many.append(outward(mid_many[2]))

    own = weighted(list(query_features), train_features, residual_weights, scale)

    in_first = inward(after(own_many[0], in_one))
    in_train.append(inward(after(train_one[half:], in_train[0])))
    mid_first = between(after(in_first, mid_many[1]))
    out_first = outward(mid_first)

    blocks_own = [0, 1, 2, 3]
    blocks_1 = [1, 2, 1, 2]
    blocks_2 = [2, 0, 3, 1]
    blocks_3 = [3, 3, 0, 0]

    checks = [jnp.where(ends, out_own[i], mid_many[i]) for i in range(most)] + [mid_one]
    found_1 = weighted(checks, train_features, residual_weights, scale)
    result_a = keepers.two_sums(own, blocks_own, found_1, blocks_1)

    beside_0 = [None, 1, 2, None]
    beside_1 = [None, 2, 1, None]
    beside_2 = [None, 3, 0, None]

    def beside(part):
        columns = slice(part * half, (part + 1) * half)

        def of(queries):
            return weighted([queries], [in_train[part]], [in_weight[columns]], scale)

        both = keepers.two_sums(of(own_one), beside_0, of(mid_one), beside_1)
        return both, of

    both_0, of_0 = beside(0)
    mid_in_one = between(after(in_one, both_0, mid_first))
    both_1, of_1 = beside(1)
    third = jnp.concatenate([of_0(mid_in_one), of_1(mid_in_one)], axis=1)
    third = keepers.sums(third, beside_2)
    both = jnp.concatenate([both_0, both_1], axis=1)
    mine_both = keepers.mine(beside_0) | keepers.mine(beside_1)
    returned = jnp.where(mine_both, both, jnp.where(keepers.mine(beside_2), third, 0.0))
    largest = jnp.maximum(jnp.max(jnp.abs(returned)), 1e-30)
    small = (returned * (16384.0 / largest)).astype(jnp.float16)

    results_b = []
    ins = [in_train[1], in_train[1]]
    for k in range(CHUNKS):
        part = slice(k * cut, (k + 1) * cut)
        got = inward(after(own_many[1:, part], ins[-2], *([result_a] if k == CHUNKS - 1 else [])))
        ins.append(got)
        mid = between(got)
        out = outward(mid)
        near_2 = [in_first[part]] + list(got)
        far_2 = [out_many[i][part] for i in range(most)]
        near_3 = [mid_first[part]] + list(mid)
        far_3 = [out_first[part]] + list(out)
        checks_2 = [jnp.where(ends, a, b) for a, b in zip(far_2, near_2)] + [in_one[part]]
        checks_3 = [jnp.where(ends, a, b) for a, b in zip(far_3, near_3)] + [mid_in_one[part]]
        found_2 = weighted(checks_2, train_features, residual_weights, scale)
        found_3 = weighted(checks_3, train_features, residual_weights, scale)
        results_b.append(keepers.two_sums(found_2, blocks_2, found_3, blocks_3))

    unit = outward(jnp.full((8, 128), largest * (1.0 / 16384.0)))
    small = outward(after(small, mid, unit))
    mine_a = keepers.mine(blocks_own) | keepers.mine(blocks_1)
    result = jnp.where(mine_a, result_a, jnp.concatenate(results_b, axis=0))
    return result + small.astype(jnp.float32) * unit[0, 0]


def local(train_features, query_features, residual_weights):
    keepers = Keepers(query_features.shape[1])
    scale = 1.0 / (train_features.shape[0] * keepers.ckpts)
    plan = line if (keepers.planes, keepers.ckpts, keepers.dims) == (4, 2, 2) else ring
    return plan(train_features, query_features, residual_weights, keepers, scale)


def solution(mesh):
    in_specs = (
        P("ckpt", ("groups", "ex"), "dim"),
        P("ckpt", ("groups", "ex"), "dim"),
        P("ckpt", ("groups", "ex")),
    )
    out_specs = P(("ckpt", "dim"), ("groups", "ex"))
    return jax.shard_map(local, mesh=mesh, in_specs=in_specs, out_specs=out_specs, check_vma=False)
```

```python
import jax
import jax.numpy as jnp
from jax import lax
from jax.sharding import PartitionSpec as P

PLACE = ("ex", "ckpt", "dim")


def after(value, *others):
    return lax.optimization_barrier((value,) + others)[0]


def weighted(checks, train, weights, scale):
    total = None
    for piece, examples, weight in zip(checks, train, weights):
        dots = lax.dot_general(
            piece,
            examples,
            (((1,), (1,)), ((), ())),
            preferred_element_type=jnp.float32,
        )
        term = dots * weight[None, :]
        total = term if total is None else total + term
    return total * scale


class Keepers:
    def __init__(self, rows):
        self.ckpts, self.dims = lax.axis_size("ckpt"), lax.axis_size("dim")
        self.planes = lax.axis_size("ex")
        self.z, self.x, self.c = [lax.axis_index(name) for name in PLACE]
        kept = rows * self.planes // (self.ckpts * self.dims)
        self.ratio = kept // rows
        assert self.ratio * rows == kept

    def index(self, z, x, c):
        return (z * self.ckpts + x) * self.dims + c

    def of(self, block):
        owner = block // self.ratio
        return owner // self.dims, owner % self.dims

    def mine(self, blocks, j=0):
        found = jnp.bool_(False)
        for z, block in enumerate(blocks):
            if block is not None and block % self.ratio == j:
                x, c = self.of(block)
                found = found | ((self.z == z) & (self.x == x) & (self.c == c))
        return found

    def sums(self, partial, blocks):
        total = partial
        for away in range(1, self.dims):
            pairs = []
            for z, block in enumerate(blocks):
                if block is not None:
                    c = self.of(block)[1]
                    for x in range(self.ckpts):
                        pairs.append((self.index(z, x, (c + away) % self.dims), self.index(z, x, c)))
            total = total + lax.ppermute(partial, PLACE, pairs)
        whole = total
        for away in range(1, self.ckpts):
            pairs = []
            for z, block in enumerate(blocks):
                if block is not None:
                    x, c = self.of(block)
                    pairs.append((self.index(z, (x + away) % self.ckpts, c), self.index(z, x, c)))
            whole = whole + lax.ppermute(total, PLACE, pairs)
        return whole

    def two_sums(self, one, one_blocks, two, two_blocks):
        keeps_one = jnp.bool_(False)
        swaps, crosses = [], []
        for z, blocks in enumerate(zip(one_blocks, two_blocks)):
            places = [None if block is None else self.of(block) for block in blocks]
            second = places[1][1]
            assert places[0] is None or places[0][1] == 1 - second
            keeps_one = keeps_one | ((self.z == z) & (self.c == 1 - second))
            for place in places:
                if place is not None:
                    at, c = place
                    swaps += [(self.index(z, x, 1 - c), self.index(z, x, c)) for x in range(2)]
                    crosses.append((self.index(z, 1 - at, c), self.index(z, at, c)))
        got = lax.ppermute(jnp.where(keeps_one, two, one), PLACE, swaps)
        total = jnp.where(keeps_one, one, two) + got
        return total + lax.ppermute(total, PLACE, crosses)


def ring(train_features, query_features, residual_weights, keepers, scale):
    planes, ratio = keepers.planes, keepers.ratio
    rows = query_features.shape[1]
    half = rows // 2
    results = [[None, None] for unused in range(ratio)]

    def finish(piece, blocks, start):
        found = weighted(list(piece), train_features, residual_weights, scale)
        whole = keepers.sums(found, blocks)
        for j in range(ratio):
            mine = keepers.mine(blocks, j)
            for k in range(found.shape[0] // half):
                part = whole[k * half:(k + 1) * half]
                at = start // half + k
                old = results[j][at]
                results[j][at] = part if old is None else jnp.where(mine, part, old)

    right = [(s, (s + 1) % planes) for s in range(planes)]
    left = [(s, (s - 1) % planes) for s in range(planes)]
    from_left = from_right = query_features
    finish(query_features, list(range(planes)), 0)
    for step in range(1, planes // 2):
        from_left = lax.ppermute(from_left, "ex", right)
        from_right = lax.ppermute(from_right, "ex", left)
        finish(from_left, [(s - step) % planes for s in range(planes)], 0)
        finish(from_right, [(s + step) % planes for s in range(planes)], 0)
    across = [(s + planes // 2) % planes for s in range(planes)]
    finish(lax.ppermute(from_left[:, :half], "ex", right), across, 0)
    finish(lax.ppermute(from_right[:, half:], "ex", left), across, half)
    return jnp.concatenate([part for block in results for part in block], axis=0)


def line(train_features, query_features, residual_weights, keepers, scale):
    z, x, c = keepers.z, keepers.x, keepers.c
    rows, depth = query_features.shape[1:]
    examples = train_features.shape[1]
    half, low = examples // 2, rows // 2
    assert train_features.shape[0] == 4 and half <= depth
    ends = (z == 0) | (z == 3)

    def inward(value):
        return lax.ppermute(value, "ex", [(0, 1), (3, 2)])

    def between(value):
        return lax.ppermute(value, "ex", [(1, 2), (2, 1)])

    def outward(value):
        return lax.ppermute(value, "ex", [(1, 0), (2, 3)])

    def scores(checks):
        return weighted(checks, train_features, residual_weights, scale)

    def chosen(far, near):
        return after(jnp.where(ends, far, near))

    def training(part):
        columns = slice(part * half, (part + 1) * half)
        left, pieces = residual_weights[0, columns], []
        for unused in range(3):
            rounded = lax.reduce_precision(left, 8, 7)
            pieces.append(rounded.astype(jnp.bfloat16))
            left = left - rounded
        tail = jnp.pad(jnp.stack(pieces), ((0, 13), (0, depth - half)))
        return jnp.concatenate([train_features[0, columns], tail], axis=0)

    out_own = outward(query_features[1:])
    in_many = inward(query_features[:3])
    mid_a = between(query_features[:2])
    own = scores(list(query_features))
    mid_b = between(after(query_features[2:], mid_a))
    out_a = outward(mid_a[1])
    in_train = [inward(after(training(0), in_many))]
    out_b = outward(mid_b)
    mid_c = between(after(in_many[:2], mid_b))
    in_train.append(inward(after(training(1), in_train[0])))

    blocks_own = [0, 1, 2, 3]
    blocks_1 = [1, 2, 1, 2]
    blocks_2 = [2, None, None, 1]
    blocks_3 = [None, 0, 3, None]
    blocks_4 = [3, 3, 0, 0]

    one = mid_a[0]
    checks = [one, chosen(out_own[0], mid_a[1])]
    later = chosen(out_own[1:], mid_b)
    found_1 = scores(checks + [later[0], later[1]])
    result_1 = keepers.two_sums(own, blocks_own, found_1, blocks_1)

    mid_d = between(after(in_many[2], mid_c))
    out_c = outward(mid_c[1])
    out_d = outward(mid_d)

    def three(part):
        block = in_train[part]
        weights = jnp.sum(block[half:half + 3, :half].astype(jnp.float32), axis=0)

        def of(queries):
            return weighted([queries], [block[:half]], [weights], scale)

        first, second, third = of(query_features[0]), of(one), of(mid_c[0])
        alone = ((z == 1) & (c == 0)) | ((z == 2) & (c == 1))
        pair = jnp.concatenate([first, third], axis=0)
        lone = jnp.concatenate([second, second], axis=0)
        swaps = [(keepers.index(p, q, r), keepers.index(p, q, 1 - r)) for p in (1, 2) for q in range(2) for r in range(2)]
        got = lax.ppermute(jnp.where(alone, pair, lone), PLACE, swaps)
        total = jnp.where(alone, lone, pair) + got
        upper, lower = total[:rows], total[rows:]
        keeps_first = keepers.mine([None, 1, 2, None])
        crosses = []
        for p, blocks in ((1, (1, 2, 3)), (2, (2, 1, 0))):
            for block in blocks:
                at, r = keepers.of(block)
                crosses.append((keepers.index(p, 1 - at, r), keepers.index(p, at, r)))
        got = lax.ppermute(jnp.where(keeps_first, lower, upper), PLACE, crosses)
        return jnp.where(keeps_first, upper, lower) + got

    ones = train_features[1:], residual_weights[1:]
    block_2 = weighted([out_a, out_b[0], out_b[1]], *ones, scale)
    result_2 = keepers.sums(block_2, blocks_2)

    last = train_features[3:], residual_weights[3:]
    base_3 = weighted(list(in_many), train_features, residual_weights, scale)
    checks = [mid_c[0], chosen(out_c, mid_c[1]), chosen(out_d, mid_d)]
    base_4 = weighted(checks, train_features, residual_weights, scale)
    results, before = [], in_train[1]
    for k in range(2):
        part = slice(k * low, (k + 1) * low)
        before = inward(after(query_features[3, part], before))
        mid = between(before)
        out = outward(mid)
        block_3 = base_3[part] + weighted([before], *last, scale)
        block_4 = base_4[part] + weighted([chosen(out, mid)], *last, scale)
        results.append(keepers.two_sums(block_3, blocks_3, block_4, blocks_4))

    returned = jnp.concatenate([three(0), three(1)], axis=1)
    returned = jnp.where(keepers.mine([None, 0, 3, None]), 0.0, returned)
    largest = jnp.clip(jnp.max(jnp.abs(returned)), 1e-30, 1e30)
    power = jnp.floor(jnp.log2(largest))
    small = (returned * jnp.exp2(13.0 - power)).astype(jnp.float16)
    small = jnp.concatenate([small, jnp.full((16, examples), power, jnp.float16)], axis=0)
    small = outward(after(small, mid))
    power = small[rows, 0].astype(jnp.float32)

    result = jnp.where(keepers.mine(blocks_2), result_2, jnp.concatenate(results, axis=0))
    result = jnp.where(keepers.mine(blocks_own) | keepers.mine(blocks_1), result_1, result)
    return result + small[:rows].astype(jnp.float32) * jnp.exp2(power - 13.0)


def local(train_features, query_features, residual_weights):
    keepers = Keepers(query_features.shape[1])
    scale = 1.0 / (train_features.shape[0] * keepers.ckpts)
    plan = line if (keepers.planes, keepers.ckpts, keepers.dims) == (4, 2, 2) else ring
    return plan(train_features, query_features, residual_weights, keepers, scale)


def solution(mesh):
    in_specs = (
        P("ckpt", ("groups", "ex"), "dim"),
        P("ckpt", ("groups", "ex"), "dim"),
        P("ckpt", ("groups", "ex")),
    )
    out_specs = P(("ckpt", "dim"), ("groups", "ex"))
    return jax.shard_map(local, mesh=mesh, in_specs=in_specs, out_specs=out_specs, check_vma=False)
```

```python
import jax
import jax.numpy as jnp
from jax import lax
from jax.sharding import PartitionSpec as P

PLACE = ("ex", "ckpt", "dim")


def after(value, *others):
    return lax.optimization_barrier((value,) + others)[0]


def weighted(checks, train, weights, scale):
    total = None
    for piece, examples, weight in zip(checks, train, weights):
        dots = lax.dot_general(
            piece,
            examples,
            (((1,), (1,)), ((), ())),
            preferred_element_type=jnp.float32,
        )
        term = dots * weight[None, :]
        total = term if total is None else total + term
    return total * scale


class Keepers:
    def __init__(self, rows):
        self.ckpts, self.dims = lax.axis_size("ckpt"), lax.axis_size("dim")
        self.planes = lax.axis_size("ex")
        self.z, self.x, self.c = [lax.axis_index(name) for name in PLACE]
        kept = rows * self.planes // (self.ckpts * self.dims)
        self.ratio = kept // rows
        assert self.ratio * rows == kept

    def index(self, z, x, c):
        return (z * self.ckpts + x) * self.dims + c

    def of(self, block):
        owner = block // self.ratio
        return owner // self.dims, owner % self.dims

    def mine(self, blocks, j=0):
        found = jnp.bool_(False)
        for z, block in enumerate(blocks):
            if block is not None and block % self.ratio == j:
                x, c = self.of(block)
                found = found | ((self.z == z) & (self.x == x) & (self.c == c))
        return found

    def sums(self, partial, blocks):
        return self.far_sums(self.near_sums(partial, blocks), blocks)

    def near_sums(self, partial, blocks):
        total = partial
        for away in range(1, self.dims):
            pairs = []
            for z, block in enumerate(blocks):
                if block is not None:
                    c = self.of(block)[1]
                    for x in range(self.ckpts):
                        pairs.append((self.index(z, x, (c + away) % self.dims), self.index(z, x, c)))
            total = total + lax.ppermute(partial, PLACE, pairs)
        return total

    def far_sums(self, total, *held):
        whole = total
        for away in range(1, self.ckpts):
            pairs = []
            for z in range(self.planes):
                for blocks in held:
                    if blocks[z] is not None:
                        x, c = self.of(blocks[z])
                        pairs.append((self.index(z, (x + away) % self.ckpts, c), self.index(z, x, c)))
            whole = whole + lax.ppermute(total, PLACE, pairs)
        return whole

    def two_near_sums(self, one, one_blocks, two, two_blocks):
        keeps_one = jnp.bool_(False)
        swaps = []
        for z, blocks in enumerate(zip(one_blocks, two_blocks)):
            second = self.of(blocks[1])[1]
            assert blocks[0] is None or self.of(blocks[0])[1] == 1 - second
            keeps_one = keeps_one | ((self.z == z) & (self.c == 1 - second))
            for block in blocks:
                if block is not None:
                    c = self.of(block)[1]
                    swaps += [(self.index(z, x, 1 - c), self.index(z, x, c)) for x in range(2)]
        got = lax.ppermute(jnp.where(keeps_one, two, one), PLACE, swaps)
        return jnp.where(keeps_one, one, two) + got


def ring(train_features, query_features, residual_weights, keepers, scale):
    planes, ratio = keepers.planes, keepers.ratio
    rows = query_features.shape[1]
    half = rows // 2
    results = [[None, None] for unused in range(ratio)]

    def finish(piece, blocks, start):
        found = weighted(list(piece), train_features, residual_weights, scale)
        whole = keepers.sums(found, blocks)
        for j in range(ratio):
            mine = keepers.mine(blocks, j)
            for k in range(found.shape[0] // half):
                part = whole[k * half:(k + 1) * half]
                at = start // half + k
                old = results[j][at]
                results[j][at] = part if old is None else jnp.where(mine, part, old)

    right = [(s, (s + 1) % planes) for s in range(planes)]
    left = [(s, (s - 1) % planes) for s in range(planes)]
    from_left = from_right = query_features
    finish(query_features, list(range(planes)), 0)
    for step in range(1, planes // 2):
        from_left = lax.ppermute(from_left, "ex", right)
        from_right = lax.ppermute(from_right, "ex", left)
        finish(from_left, [(s - step) % planes for s in range(planes)], 0)
        finish(from_right, [(s + step) % planes for s in range(planes)], 0)
    across = [(s + planes // 2) % planes for s in range(planes)]
    finish(lax.ppermute(from_left[:, :half], "ex", right), across, 0)
    finish(lax.ppermute(from_right[:, half:], "ex", left), across, half)
    return jnp.concatenate([part for block in results for part in block], axis=0)


def packed(value):
    largest = jnp.clip(jnp.max(jnp.abs(value)), 1e-30, 1e30)
    power = jnp.floor(jnp.log2(largest))
    small = (value * jnp.exp2(13.0 - power)).astype(jnp.float16)
    return jnp.concatenate([small, jnp.full((16, value.shape[1]), power, jnp.float16)], axis=0)


def unpacked(small):
    power = small[-16, 0].astype(jnp.float32)
    return small[:-16].astype(jnp.float32) * jnp.exp2(power - 13.0)


def line(train_features, query_features, residual_weights, keepers, scale):
    z, c = keepers.z, keepers.c
    rows, depth = query_features.shape[1:]
    examples = train_features.shape[1]
    low = rows // 2
    assert train_features.shape[0] == 4 and examples <= depth
    ends = (z == 0) | (z == 3)

    def inward(value):
        return lax.ppermute(value, "ex", [(0, 1), (3, 2)])

    def between(value):
        return lax.ppermute(value, "ex", [(1, 2), (2, 1)])

    def outward(value):
        return lax.ppermute(value, "ex", [(1, 0), (2, 3)])

    def scores(checks, first=0):
        return weighted(checks, train_features[first:], residual_weights[first:], scale)

    def chosen(far, near):
        return after(jnp.where(ends, far, near))

    left, pieces = residual_weights[0], []
    for unused in range(3):
        rounded = lax.reduce_precision(left, 8, 7)
        pieces.append(rounded.astype(jnp.bfloat16))
        left = left - rounded
    tail = jnp.pad(jnp.stack(pieces), ((0, 13), (0, depth - examples)))
    training = jnp.concatenate([train_features[0], tail], axis=0)

    in_many = inward(query_features[:3])
    mid_own = between(query_features[1:])
    out_own = outward(query_features[1:])
    own = scores(list(query_features))
    out_next = outward(mid_own)
    mid_edge = between(after(in_many[1:], mid_own))
    in_train = inward(after(training, in_many))
    out_edge = outward(mid_edge)
    mid_first = between(after(jnp.stack([query_features[0], in_many[0]]), mid_edge))
    one, far_one = mid_first[0], mid_first[1]

    blocks_own = [0, 1, 2, 3]
    blocks_1 = [1, 2, 1, 2]
    blocks_2 = [2, None, None, 1]
    blocks_3 = [None, 0, 3, None]
    blocks_4 = [3, 3, 0, 0]

    checks = chosen(after(out_own, in_many), mid_own)
    found_1 = scores(list(checks), 1)
    found_2 = scores(list(after(out_next, mid_edge)), 1)
    total_2 = keepers.near_sums(found_2, blocks_2)
    result_2 = keepers.far_sums(total_2, blocks_2)

    weights = jnp.sum(in_train[examples:examples + 3, :examples].astype(jnp.float32), axis=0)

    def beside(queries):
        return weighted([queries], [in_train[:examples]], [weights], scale)

    first, second, third = beside(query_features[0]), beside(one), beside(far_one)
    alone = ((z == 1) & (c == 0)) | ((z == 2) & (c == 1))
    pair = jnp.concatenate([first, third], axis=0)
    lone = jnp.concatenate([second, second], axis=0)
    swaps = [(keepers.index(p, q, r), keepers.index(p, q, 1 - r)) for p in (1, 2) for q in range(2) for r in range(2)]
    got = lax.ppermute(jnp.where(alone, pair, lone), PLACE, swaps)
    total = jnp.where(alone, lone, pair) + got
    keeps_first = keepers.mine([None, 1, 2, None])
    crosses = []
    for p, blocks in ((1, (1, 2, 3)), (2, (2, 1, 0))):
        for block in blocks:
            at, r = keepers.of(block)
            crosses.append((keepers.index(p, 1 - at, r), keepers.index(p, at, r)))
    crossing = packed(jnp.where(keeps_first, total[rows:], total[:rows]))
    got = lax.ppermute(crossing, PLACE, crosses)
    returned = jnp.where(keeps_first, total[:rows], total[rows:]) + unpacked(got)
    returned = packed(jnp.where(keepers.mine([None, 0, 3, None]), 0.0, returned))

    found_1 = found_1 + scores([one])
    total_1 = keepers.two_near_sums(own, blocks_own, found_1, blocks_1)
    result_1 = keepers.far_sums(total_1, blocks_own, blocks_1)

    base_3 = scores(list(in_many))
    checks = chosen(after(out_edge, in_train), mid_edge)
    base_4 = scores([far_one, checks[0], checks[1]])
    results, before = [], in_train
    for k in range(2):
        part = slice(k * low, (k + 1) * low)
        before = inward(after(query_features[3, part], before, total_2))
        mid = between(after(before, total_1 if k == 0 else crossing))
        out = outward(mid)
        block_3 = base_3[part] + scores([before], 3)
        block_4 = base_4[part] + scores([chosen(out, mid)], 3)
        total = keepers.two_near_sums(block_3, blocks_3, block_4, blocks_4)
        results.append(keepers.far_sums(total, blocks_3, blocks_4))
    returned = unpacked(outward(after(returned, mid)))

    result = jnp.where(keepers.mine(blocks_2), result_2, jnp.concatenate(results, axis=0))
    result = jnp.where(keepers.mine(blocks_own) | keepers.mine(blocks_1), result_1, result)
    return result + returned


def local(train_features, query_features, residual_weights):
    keepers = Keepers(query_features.shape[1])
    scale = 1.0 / (train_features.shape[0] * keepers.ckpts)
    plan = line if (keepers.planes, keepers.ckpts, keepers.dims) == (4, 2, 2) else ring
    return plan(train_features, query_features, residual_weights, keepers, scale)


def solution(mesh):
    in_specs = (
        P("ckpt", ("groups", "ex"), "dim"),
        P("ckpt", ("groups", "ex"), "dim"),
        P("ckpt", ("groups", "ex")),
    )
    out_specs = P(("ckpt", "dim"), ("groups", "ex"))
    return jax.shard_map(local, mesh=mesh, in_specs=in_specs, out_specs=out_specs, check_vma=False)
```

```python
import jax
import jax.numpy as jnp
from jax import lax
from jax.sharding import PartitionSpec as P

PLACE = ("ex", "ckpt", "dim")


def after(value, *others):
    return lax.optimization_barrier((value,) + others)[0]


def weighted(checks, train, weights, scale):
    total = None
    for piece, examples, weight in zip(checks, train, weights):
        dots = lax.dot_general(
            piece,
            examples,
            (((1,), (1,)), ((), ())),
            preferred_element_type=jnp.float32,
        )
        term = dots * weight[None, :]
        total = term if total is None else total + term
    return total * scale


class Keepers:
    def __init__(self, rows):
        self.ckpts, self.dims = lax.axis_size("ckpt"), lax.axis_size("dim")
        self.planes = lax.axis_size("ex")
        self.z, self.x, self.c = [lax.axis_index(name) for name in PLACE]
        kept = rows * self.planes // (self.ckpts * self.dims)
        self.ratio = kept // rows
        assert self.ratio * rows == kept

    def index(self, z, x, c):
        return (z * self.ckpts + x) * self.dims + c

    def of(self, block):
        owner = block // self.ratio
        return owner // self.dims, owner % self.dims

    def mine(self, blocks, j=0):
        found = jnp.bool_(False)
        for z, block in enumerate(blocks):
            if block is not None and block % self.ratio == j:
                x, c = self.of(block)
                found = found | ((self.z == z) & (self.x == x) & (self.c == c))
        return found

    def sums(self, partial, blocks):
        return self.far_sums(self.near_sums(partial, blocks), blocks)

    def near_sums(self, partial, blocks):
        total = partial
        for away in range(1, self.dims):
            pairs = []
            for z, block in enumerate(blocks):
                if block is not None:
                    c = self.of(block)[1]
                    for x in range(self.ckpts):
                        pairs.append((self.index(z, x, (c + away) % self.dims), self.index(z, x, c)))
            total = total + lax.ppermute(partial, PLACE, pairs)
        return total

    def far_sums(self, total, *held):
        whole = total
        for away in range(1, self.ckpts):
            whole = whole + self.far_moves(total, *held, away=away)
        return whole

    def far_moves(self, total, *held, away=1):
        pairs = []
        for z in range(self.planes):
            for blocks in held:
                if blocks[z] is not None:
                    x, c = self.of(blocks[z])
                    pairs.append((self.index(z, (x + away) % self.ckpts, c), self.index(z, x, c)))
        return lax.ppermute(total, PLACE, pairs)

    def two_near_sums(self, one, one_blocks, two, two_blocks):
        keeps_one = jnp.bool_(False)
        swaps = []
        for z, blocks in enumerate(zip(one_blocks, two_blocks)):
            if blocks[0] is None:
                continue
            second = self.of(blocks[1])[1]
            assert self.of(blocks[0])[1] == 1 - second
            keeps_one = keeps_one | ((self.z == z) & (self.c == 1 - second))
            swaps += [(self.index(z, x, c), self.index(z, x, 1 - c)) for x in range(2) for c in range(2)]
        got = lax.ppermute(jnp.where(keeps_one, two, one), PLACE, swaps)
        return jnp.where(keeps_one, one, two) + got


def ring(train_features, query_features, residual_weights, keepers, scale):
    planes, ratio = keepers.planes, keepers.ratio
    rows = query_features.shape[1]
    half = rows // 2
    results = [[None, None] for unused in range(ratio)]

    def finish(piece, blocks, start):
        found = weighted(list(piece), train_features, residual_weights, scale)
        whole = keepers.sums(found, blocks)
        for j in range(ratio):
            mine = keepers.mine(blocks, j)
            for k in range(found.shape[0] // half):
                part = whole[k * half:(k + 1) * half]
                at = start // half + k
                old = results[j][at]
                results[j][at] = part if old is None else jnp.where(mine, part, old)

    right = [(s, (s + 1) % planes) for s in range(planes)]
    left = [(s, (s - 1) % planes) for s in range(planes)]
    from_left = from_right = query_features
    finish(query_features, list(range(planes)), 0)
    for step in range(1, planes // 2):
        from_left = lax.ppermute(from_left, "ex", right)
        from_right = lax.ppermute(from_right, "ex", left)
        finish(from_left, [(s - step) % planes for s in range(planes)], 0)
        finish(from_right, [(s + step) % planes for s in range(planes)], 0)
    across = [(s + planes // 2) % planes for s in range(planes)]
    finish(lax.ppermute(from_left[:, :half], "ex", right), across, 0)
    finish(lax.ppermute(from_right[:, half:], "ex", left), across, half)
    return jnp.concatenate([part for block in results for part in block], axis=0)


def packed(value):
    largest = jnp.clip(jnp.max(jnp.abs(value)), 1e-30, 1e30)
    power = jnp.floor(jnp.log2(largest))
    small = (value * jnp.exp2(13.0 - power)).astype(jnp.float16)
    return jnp.concatenate([small, jnp.full((16, value.shape[1]), power, jnp.float16)], axis=0)


def unpacked(small):
    power = small[-16, 0].astype(jnp.float32)
    return small[:-16].astype(jnp.float32) * jnp.exp2(power - 13.0)


def line(train_features, query_features, residual_weights, keepers, scale):
    z = keepers.z
    rows, depth = query_features.shape[1:]
    examples = train_features.shape[1]
    low = rows // 2
    assert train_features.shape[0] == 4 and examples <= depth
    ends = (z == 0) | (z == 3)

    def aside(value):
        return lax.ppermute(value, "ex", [(0, 1), (1, 0), (2, 3), (3, 2)])

    def inward(value):
        return lax.ppermute(value, "ex", [(0, 1), (3, 2)])

    def between(value):
        return lax.ppermute(value, "ex", [(1, 2), (2, 1)])

    def outward(value):
        return lax.ppermute(value, "ex", [(1, 0), (2, 3)])

    def scores(checks, first=0):
        return weighted(checks, train_features[first:], residual_weights[first:], scale)

    def chosen(far, near):
        return after(jnp.where(ends, far, near))

    left, pieces = residual_weights[0], []
    for unused in range(3):
        rounded = lax.reduce_precision(left, 8, 7)
        pieces.append(rounded.astype(jnp.bfloat16))
        left = left - rounded
    tail = jnp.pad(jnp.stack(pieces), ((0, 13), (0, depth - examples)))
    training = jnp.concatenate([train_features[0], tail], axis=0)

    side = aside(query_features)
    middle = between(query_features)
    own = scores(list(query_features))
    in_train = inward(after(training, side))
    out_next = outward(middle[1:])
    parts = [slice(0, low), slice(low, rows)]
    blocks_own = [0, 1, 2, 3]
    blocks_1 = [1, 0, 3, 2]
    blocks_2 = [2, 2, 1, 1]
    blocks_3 = [3, 3, 0, 0]

    total_1 = keepers.two_near_sums(own, blocks_own, scores(list(side)), blocks_1)
    result_1 = keepers.far_sums(total_1, blocks_own, blocks_1)

    mid_edge = [between(side[1:, parts[0]])]
    mid_edge.append(between(after(side[1:, parts[1]], mid_edge[0], total_1)))
    out_edge = [outward(part) for part in mid_edge]
    far_one = between(after(side[0], mid_edge[1]))

    checks = chosen(out_next, middle[1:])
    total_2 = keepers.near_sums(scores([middle[0]] + list(checks)), blocks_2)
    result_2 = keepers.far_sums(total_2, blocks_2)

    weights = jnp.sum(in_train[examples:examples + 3, :examples].astype(jnp.float32), axis=0)

    def beside(queries):
        return weighted([queries], [in_train[:examples]], [weights], scale)

    beside_2 = [None, 2, 1, None]
    beside_3 = [None, 3, 0, None]
    total = keepers.two_near_sums(beside(middle[0]), beside_2, beside(far_one), beside_3)
    crossing = packed(after(total, result_1, total_2))
    returned = total + unpacked(keepers.far_moves(crossing, beside_2, beside_3))
    returned = jnp.where(keepers.mine(beside_2) | keepers.mine(beside_3), returned, 0.0)

    def last(k, *before):
        checks = chosen(after(out_edge[k], *before), mid_edge[k])
        found = scores([far_one[parts[k]]] + list(checks))
        return keepers.near_sums(found, blocks_3)

    total_3 = [last(0, crossing)]
    results = [keepers.far_sums(total_3[0], blocks_3)]
    returned = packed(after(returned, result_2, total_3[0]))
    halves = [after(jnp.concatenate([returned[part], returned[rows:]], axis=0)) for part in parts]
    total_3.append(last(1, *halves))
    halves = [outward(half) for half in halves]
    results.append(keepers.far_sums(after(total_3[1], halves[0]), blocks_3))
    returned = jnp.concatenate([unpacked(part) for part in halves], axis=0)

    result = jnp.where(keepers.mine(blocks_2), result_2, jnp.concatenate(results, axis=0))
    result = jnp.where(keepers.mine(blocks_own) | keepers.mine(blocks_1), result_1, result)
    return result + returned


def local(train_features, query_features, residual_weights):
    keepers = Keepers(query_features.shape[1])
    scale = 1.0 / (train_features.shape[0] * keepers.ckpts)
    plan = line if (keepers.planes, keepers.ckpts, keepers.dims) == (4, 2, 2) else ring
    return plan(train_features, query_features, residual_weights, keepers, scale)


def solution(mesh):
    in_specs = (
        P("ckpt", ("groups", "ex"), "dim"),
        P("ckpt", ("groups", "ex"), "dim"),
        P("ckpt", ("groups", "ex")),
    )
    out_specs = P(("ckpt", "dim"), ("groups", "ex"))
    return jax.shard_map(local, mesh=mesh, in_specs=in_specs, out_specs=out_specs, check_vma=False)
```

```python
import functools

import jax
import jax.numpy as jnp
from jax import lax
from jax.experimental import pallas as pl
from jax.experimental.pallas import tpu as pltpu
from jax.sharding import PartitionSpec as P

PLACE = ("ex", "ckpt", "dim")
VMEM = 48 * 1024 * 1024


def after(value, *others):
    return lax.optimization_barrier((value,) + others)[0]


def weighted(checks, train, weights, scale):
    total = None
    for piece, examples, weight in zip(checks, train, weights):
        dots = lax.dot_general(
            piece,
            examples,
            (((1,), (1,)), ((), ())),
            preferred_element_type=jnp.float32,
        )
        term = dots * weight[None, :]
        total = term if total is None else total + term
    return total * scale


class Keepers:
    def __init__(self, rows):
        self.ckpts, self.dims = lax.axis_size("ckpt"), lax.axis_size("dim")
        self.planes = lax.axis_size("ex")
        self.z, self.x, self.c = [lax.axis_index(name) for name in PLACE]
        kept = rows * self.planes // (self.ckpts * self.dims)
        self.ratio = kept // rows
        assert self.ratio * rows == kept

    def index(self, z, x, c):
        return (z * self.ckpts + x) * self.dims + c

    def of(self, block):
        owner = block // self.ratio
        return owner // self.dims, owner % self.dims

    def mine(self, blocks, j=0):
        found = jnp.bool_(False)
        for z, block in enumerate(blocks):
            if block is not None and block % self.ratio == j:
                x, c = self.of(block)
                found = found | ((self.z == z) & (self.x == x) & (self.c == c))
        return found

    def sums(self, partial, blocks):
        return self.far_sums(self.near_sums(partial, blocks), blocks)

    def near_sums(self, partial, blocks):
        total = partial
        for away in range(1, self.dims):
            pairs = []
            for z, block in enumerate(blocks):
                if block is not None:
                    c = self.of(block)[1]
                    for x in range(self.ckpts):
                        pairs.append((self.index(z, x, (c + away) % self.dims), self.index(z, x, c)))
            total = total + lax.ppermute(partial, PLACE, pairs)
        return total

    def far_sums(self, total, *held):
        whole = total
        for away in range(1, self.ckpts):
            whole = whole + self.far_moves(total, *held, away=away)
        return whole

    def far_moves(self, total, *held, away=1):
        pairs = []
        for z in range(self.planes):
            for blocks in held:
                if blocks[z] is not None:
                    x, c = self.of(blocks[z])
                    pairs.append((self.index(z, (x + away) % self.ckpts, c), self.index(z, x, c)))
        return lax.ppermute(total, PLACE, pairs)

    def keeps_first(self, blocks):
        found = jnp.bool_(False)
        for z, block in enumerate(blocks):
            if block is not None:
                found = found | ((self.z == z) & (self.c == self.of(block)[1]))
        return found

    def swapped(self, value, planes):
        pairs = []
        for z in planes:
            for x in range(self.ckpts):
                pairs += [(self.index(z, x, c), self.index(z, x, 1 - c)) for c in range(2)]
        return lax.ppermute(value, PLACE, pairs)


def ring(train_features, query_features, residual_weights, keepers, scale):
    planes, ratio = keepers.planes, keepers.ratio
    rows = query_features.shape[1]
    half = rows // 2
    results = [[None, None] for unused in range(ratio)]

    def finish(piece, blocks, start):
        found = weighted(list(piece), train_features, residual_weights, scale)
        whole = keepers.sums(found, blocks)
        for j in range(ratio):
            mine = keepers.mine(blocks, j)
            for k in range(found.shape[0] // half):
                part = whole[k * half:(k + 1) * half]
                at = start // half + k
                old = results[j][at]
                results[j][at] = part if old is None else jnp.where(mine, part, old)

    right = [(s, (s + 1) % planes) for s in range(planes)]
    left = [(s, (s - 1) % planes) for s in range(planes)]
    from_left = from_right = query_features
    finish(query_features, list(range(planes)), 0)
    for step in range(1, planes // 2):
        from_left = lax.ppermute(from_left, "ex", right)
        from_right = lax.ppermute(from_right, "ex", left)
        finish(from_left, [(s - step) % planes for s in range(planes)], 0)
        finish(from_right, [(s + step) % planes for s in range(planes)], 0)
    across = [(s + planes // 2) % planes for s in range(planes)]
    finish(lax.ppermute(from_left[:, :half], "ex", right), across, 0)
    finish(lax.ppermute(from_right[:, half:], "ex", left), across, half)
    return jnp.concatenate([part for block in results for part in block], axis=0)


def packed(value):
    largest = jnp.clip(jnp.max(jnp.abs(value)), 1e-30, 1e30)
    power = jnp.floor(jnp.log2(largest))
    small = (value * jnp.exp2(13.0 - power)).astype(jnp.float16)
    return jnp.concatenate([small, jnp.full((16, value.shape[1]), power, jnp.float16)], axis=0)


def unpacked(small):
    power = small[-16, 0].astype(jnp.float32)
    return small[:-16].astype(jnp.float32) * jnp.exp2(power - 13.0)


def product(queries, examples):
    return lax.dot_general(
        queries,
        examples,
        (((1,), (1,)), ((), ())),
        preferred_element_type=jnp.float32,
    )


def pair_kernel(scale, flag_ref, one_ref, two_ref, train_ref, weight_ref, sent_ref, kept_ref):
    keeps_one = flag_ref[0] == 1
    sent = kept = None
    for check in range(train_ref.shape[0]):
        one, two = one_ref[check], two_ref[check]
        weight = jnp.sum(weight_ref[check].astype(jnp.float32), axis=0, keepdims=True)
        both = []
        for first, second in ((two, one), (one, two)):
            term = product(jnp.where(keeps_one, first, second), train_ref[check]) * weight
            both.append(term)
        sent = both[0] if sent is None else sent + both[0]
        kept = both[1] if kept is None else kept + both[1]
    sent_ref[...] = sent * scale
    kept_ref[...] = kept * scale


def pair_scores(keeps_one, one, two, train, weights, scale, examples):
    checks, rows, depth = one.shape
    tile = 256
    return pl.pallas_call(
        functools.partial(pair_kernel, scale),
        grid_spec=pltpu.PrefetchScalarGridSpec(
            num_scalar_prefetch=1,
            grid=(examples // tile,),
            in_specs=[
                pl.BlockSpec((checks, rows, depth), lambda i, flag: (0, 0, 0)),
                pl.BlockSpec((checks, rows, depth), lambda i, flag: (0, 0, 0)),
                pl.BlockSpec((checks, tile, depth), lambda i, flag: (0, i, 0)),
                pl.BlockSpec((checks, weights.shape[1], tile), lambda i, flag: (0, 0, i)),
            ],
            out_specs=[pl.BlockSpec((rows, tile), lambda i, flag: (0, i))] * 2,
        ),
        out_shape=[jax.ShapeDtypeStruct((rows, examples), jnp.float32)] * 2,
        compiler_params=pltpu.CompilerParams(vmem_limit_bytes=VMEM),
        cost_estimate=pl.CostEstimate(flops=0, bytes_accessed=0, transcendentals=0),
    )(keeps_one.astype(jnp.int32).reshape(1), one, two, train, weights)


def block_kernel(scale, flag_ref, far_ref, near_ref, first_ref, train_ref, weight_ref, out_ref):
    is_end = flag_ref[0] == 1
    total = product(first_ref[...], train_ref[0]) * weight_ref[0]
    for check in range(1, train_ref.shape[0]):
        queries = jnp.where(is_end, far_ref[check - 1], near_ref[check - 1])
        total = total + product(queries, train_ref[check]) * weight_ref[check]
    out_ref[...] = total * scale


def block_scores(is_end, far, near, first, train, weights, scale):
    checks, rows, depth = far.shape
    examples, tile = train.shape[1], 256
    whole = pl.BlockSpec((checks, rows, depth), lambda i, flag: (0, 0, 0))
    return pl.pallas_call(
        functools.partial(block_kernel, scale),
        grid_spec=pltpu.PrefetchScalarGridSpec(
            num_scalar_prefetch=1,
            grid=(examples // tile,),
            in_specs=[
                whole,
                whole,
                pl.BlockSpec((rows, depth), lambda i, flag: (0, 0)),
                pl.BlockSpec((checks + 1, tile, depth), lambda i, flag: (0, i, 0)),
                pl.BlockSpec((checks + 1, 1, tile), lambda i, flag: (0, 0, i)),
            ],
            out_specs=pl.BlockSpec((rows, tile), lambda i, flag: (0, i)),
        ),
        out_shape=jax.ShapeDtypeStruct((rows, examples), jnp.float32),
        compiler_params=pltpu.CompilerParams(vmem_limit_bytes=VMEM),
        cost_estimate=pl.CostEstimate(flops=0, bytes_accessed=0, transcendentals=0),
    )(is_end.astype(jnp.int32).reshape(1), far, near, first, train, weights)


def line(train_features, query_features, residual_weights, keepers, scale):
    z = keepers.z
    rows, depth = query_features.shape[1:]
    examples = train_features.shape[1]
    assert train_features.shape[0] == 4 and examples <= depth and examples % 256 == 0
    ends = (z == 0) | (z == 3)

    def aside(value):
        return lax.ppermute(value, "ex", [(0, 1), (1, 0), (2, 3), (3, 2)])

    def inward(value):
        return lax.ppermute(value, "ex", [(0, 1), (3, 2)])

    def between(value):
        return lax.ppermute(value, "ex", [(1, 2), (2, 1)])

    def outward(value):
        return lax.ppermute(value, "ex", [(1, 0), (2, 3)])

    left, pieces = residual_weights[0], []
    for unused in range(3):
        rounded = lax.reduce_precision(left, 8, 7)
        pieces.append(rounded.astype(jnp.bfloat16))
        left = left - rounded
    tail = jnp.pad(jnp.stack(pieces), ((0, 13), (0, depth - examples)))
    training = jnp.concatenate([train_features[0], tail], axis=0)
    weights = residual_weights[:, None]

    side = aside(query_features)
    middle = between(query_features)
    in_train = inward(after(training, side))
    out_next = outward(middle[1:])
    mid_edge = between(side[1:])
    out_edge = [outward(mid_edge[:1])]
    out_edge.append(outward(after(mid_edge[1:], out_edge[0])))
    blocks_own = [0, 1, 2, 3]
    blocks_1 = [1, 0, 3, 2]
    blocks_2 = [2, 2, 1, 1]
    blocks_3 = [3, 3, 0, 0]

    sent, kept = pair_scores(
        keepers.keeps_first(blocks_own), query_features, side, train_features, weights, scale, examples)
    total_1 = kept + keepers.swapped(sent, range(4))
    result_1 = keepers.far_sums(total_1, blocks_own, blocks_1)
    far_one = between(after(side[0], mid_edge, total_1))

    found = block_scores(ends, out_next, middle[1:], middle[0], train_features, weights, scale)
    total_2 = keepers.near_sums(found, blocks_2)
    result_2 = keepers.far_sums(total_2, blocks_2)

    beside_2 = [None, 2, 1, None]
    beside_3 = [None, 3, 0, None]
    in_train = after(in_train, total_2)
    sent, kept = pair_scores(
        keepers.keeps_first(beside_2), middle[:1], far_one[None], in_train[None],
        in_train[None, examples:examples + 3, :examples], scale, examples)
    total = kept + keepers.swapped(sent, (1, 2))
    crossing = after(packed(after(total, result_1, out_edge[0])))
    returned = total + unpacked(keepers.far_moves(crossing, beside_2, beside_3))
    returned = jnp.where(keepers.mine(beside_2) | keepers.mine(beside_3), returned, 0.0)
    returned = after(packed(after(returned, result_2)))
    out_edge = after(jnp.concatenate(out_edge, axis=0), crossing)
    returned = unpacked(outward(returned))

    found = block_scores(ends, out_edge, mid_edge, far_one, train_features, weights, scale)
    result_3 = keepers.far_sums(keepers.near_sums(found, blocks_3), blocks_3)

    result = jnp.where(keepers.mine(blocks_2), result_2, result_3)
    result = jnp.where(keepers.mine(blocks_own) | keepers.mine(blocks_1), result_1, result)
    return result + returned


def local(train_features, query_features, residual_weights):
    keepers = Keepers(query_features.shape[1])
    scale = 1.0 / (train_features.shape[0] * keepers.ckpts)
    plan = line if (keepers.planes, keepers.ckpts, keepers.dims) == (4, 2, 2) else ring
    return plan(train_features, query_features, residual_weights, keepers, scale)


def solution(mesh):
    in_specs = (
        P("ckpt", ("groups", "ex"), "dim"),
        P("ckpt", ("groups", "ex"), "dim"),
        P("ckpt", ("groups", "ex")),
    )
    out_specs = P(("ckpt", "dim"), ("groups", "ex"))
    return jax.shard_map(local, mesh=mesh, in_specs=in_specs, out_specs=out_specs, check_vma=False)
```

```python
import functools

import jax
import jax.numpy as jnp
from jax import lax
from jax.experimental import pallas as pl
from jax.experimental.pallas import tpu as pltpu
from jax.sharding import PartitionSpec as P

PLACE = ("ex", "ckpt", "dim")
VMEM = 48 * 1024 * 1024


def after(value, *others):
    return lax.optimization_barrier((value,) + others)[0]


class Keepers:
    def __init__(self, rows):
        self.ckpts, self.dims = lax.axis_size("ckpt"), lax.axis_size("dim")
        self.planes = lax.axis_size("ex")
        self.z, self.x, self.c = [lax.axis_index(name) for name in PLACE]
        kept = rows * self.planes // (self.ckpts * self.dims)
        self.ratio = kept // rows
        assert self.ratio * rows == kept

    def index(self, z, x, c):
        return (z * self.ckpts + x) * self.dims + c

    def of(self, block):
        owner = block // self.ratio
        return owner // self.dims, owner % self.dims

    def mine(self, blocks, j=0):
        found = jnp.bool_(False)
        for z, block in enumerate(blocks):
            if block is not None and block % self.ratio == j:
                x, c = self.of(block)
                found = found | ((self.z == z) & (self.x == x) & (self.c == c))
        return found

    def sums(self, partial, blocks):
        return self.far_sums(self.near_sums(partial, blocks), blocks)

    def near_sums(self, partial, blocks):
        total = partial
        for away in range(1, self.dims):
            pairs = []
            for z, block in enumerate(blocks):
                if block is not None:
                    c = self.of(block)[1]
                    for x in range(self.ckpts):
                        pairs.append((self.index(z, x, (c + away) % self.dims), self.index(z, x, c)))
            total = total + lax.ppermute(partial, PLACE, pairs)
        return total

    def far_sums(self, total, *held):
        whole = total
        for away in range(1, self.ckpts):
            whole = whole + self.far_moves(total, *held, away=away)
        return whole

    def far_moves(self, total, *held, away=1):
        pairs = []
        for z in range(self.planes):
            for blocks in held:
                if blocks[z] is not None:
                    x, c = self.of(blocks[z])
                    pairs.append((self.index(z, (x + away) % self.ckpts, c), self.index(z, x, c)))
        return lax.ppermute(total, PLACE, pairs)

    def keeps_first(self, blocks):
        found = jnp.bool_(False)
        for z, block in enumerate(blocks):
            if block is not None:
                found = found | ((self.z == z) & (self.c == self.of(block)[1]))
        return found

    def swapped(self, value, planes):
        pairs = []
        for z in planes:
            for x in range(self.ckpts):
                pairs += [(self.index(z, x, c), self.index(z, x, 1 - c)) for c in range(2)]
        return lax.ppermute(value, PLACE, pairs)


def product(queries, examples):
    return lax.dot_general(
        queries,
        examples,
        (((1,), (1,)), ((), ())),
        preferred_element_type=jnp.float32,
    )


def pair_kernel(scale, flag_ref, one_ref, two_ref, train_ref, weight_ref, sent_ref, kept_ref):
    keeps_one = flag_ref[0] == 1
    sent = kept = None
    for check in range(train_ref.shape[0]):
        one, two = one_ref[check], two_ref[check]
        weight = jnp.sum(weight_ref[check].astype(jnp.float32), axis=0, keepdims=True)
        both = []
        for first, second in ((two, one), (one, two)):
            term = product(jnp.where(keeps_one, first, second), train_ref[check]) * weight
            both.append(term)
        sent = both[0] if sent is None else sent + both[0]
        kept = both[1] if kept is None else kept + both[1]
    sent_ref[...] = sent * scale
    kept_ref[...] = kept * scale


def pair_scores(keeps_one, one, two, train, weights, scale, examples):
    checks, rows, depth = one.shape
    tile = 256
    return pl.pallas_call(
        functools.partial(pair_kernel, scale),
        grid_spec=pltpu.PrefetchScalarGridSpec(
            num_scalar_prefetch=1,
            grid=(examples // tile,),
            in_specs=[
                pl.BlockSpec((checks, rows, depth), lambda i, flag: (0, 0, 0)),
                pl.BlockSpec((checks, rows, depth), lambda i, flag: (0, 0, 0)),
                pl.BlockSpec((checks, tile, depth), lambda i, flag: (0, i, 0)),
                pl.BlockSpec((checks, weights.shape[1], tile), lambda i, flag: (0, 0, i)),
            ],
            out_specs=[pl.BlockSpec((rows, tile), lambda i, flag: (0, i))] * 2,
        ),
        out_shape=[jax.ShapeDtypeStruct((rows, examples), jnp.float32)] * 2,
        compiler_params=pltpu.CompilerParams(vmem_limit_bytes=VMEM),
        cost_estimate=pl.CostEstimate(flops=0, bytes_accessed=0, transcendentals=0),
    )(keeps_one.astype(jnp.int32).reshape(1), one, two, train, weights)


def block_kernel(scale, queries_ref, train_ref, weight_ref, out_ref):
    total = None
    for check in range(train_ref.shape[0]):
        term = product(queries_ref[check], train_ref[check]) * weight_ref[check]
        total = term if total is None else total + term
    out_ref[...] = total * scale


def block_scores(queries, train, weights, scale):
    checks, rows, depth = queries.shape
    examples, tile = train.shape[1], 256
    return pl.pallas_call(
        functools.partial(block_kernel, scale),
        grid=(examples // tile,),
        in_specs=[
            pl.BlockSpec((checks, rows, depth), lambda i: (0, 0, 0)),
            pl.BlockSpec((checks, tile, depth), lambda i: (0, i, 0)),
            pl.BlockSpec((checks, 1, tile), lambda i: (0, 0, i)),
        ],
        out_specs=pl.BlockSpec((rows, tile), lambda i: (0, i)),
        out_shape=jax.ShapeDtypeStruct((rows, examples), jnp.float32),
        compiler_params=pltpu.CompilerParams(vmem_limit_bytes=VMEM),
        cost_estimate=pl.CostEstimate(flops=0, bytes_accessed=0, transcendentals=0),
    )(queries, train, weights)


def ring(train_features, query_features, residual_weights, keepers, scale):
    planes, ratio = keepers.planes, keepers.ratio
    rows = query_features.shape[1]
    cut = rows // 4
    weights = residual_weights[:, None]
    right = [(s, (s + 1) % planes) for s in range(planes)]
    left = [(s, (s - 1) % planes) for s in range(planes)]

    def blocks_at(step):
        return [(s + step) % planes for s in range(planes)]

    def one_block(queries, step):
        found = block_scores(queries, train_features, weights, scale)
        return keepers.sums(found, blocks_at(step))

    def chosen(parts):
        found = []
        for j in range(ratio):
            kept = None
            for step, whole in parts:
                mine = keepers.mine(blocks_at(step), j)
                kept = whole if kept is None else jnp.where(mine, whole, kept)
            found.append(kept)
        return found

    from_left = from_right = query_features
    whole, parts = None, []
    for step in range(1, planes // 2):
        from_right = lax.ppermute(from_right, "ex", left)
        from_left = lax.ppermute(from_left, "ex", right)
        if step < planes // 2 - 1:
            parts += [(step, one_block(from_right, step)), (-step, one_block(from_left, -step))]
    low = lax.ppermute(from_right[:, cut:], "ex", left)
    step = planes // 2 - 1
    own = after(query_features, from_right)
    if keepers.dims == 2 and ratio == 1 and step == 1:
        sent, kept = pair_scores(
            keepers.keeps_first(blocks_at(0)), own, from_right, train_features, weights, scale,
            train_features.shape[1])
        total = kept + keepers.swapped(sent, range(planes))
        ahead = keepers.far_sums(total, blocks_at(0), blocks_at(1))
        parts += [(0, ahead), (1, ahead)]
    else:
        ahead = one_block(from_right, step)
        parts += [(0, one_block(own, 0)), (step, ahead)]
    top = lax.ppermute(after(from_left[:, :cut], low), "ex", right)
    behind = one_block(after(from_left, low, ahead), -step)
    parts.append((-step, behind))
    below = one_block(low, planes // 2)
    above = one_block(after(top, behind, below), planes // 2)
    tops = chosen([(step, part[:cut]) for step, part in parts] + [(planes // 2, above)])
    lows = chosen([(step, part[cut:]) for step, part in parts] + [(planes // 2, below)])
    return jnp.concatenate([part for both in zip(tops, lows) for part in both], axis=0)


def local(train_features, query_features, residual_weights):
    keepers = Keepers(query_features.shape[1])
    scale = 1.0 / (train_features.shape[0] * keepers.ckpts)
    return ring(train_features, query_features, residual_weights, keepers, scale)


def solution(mesh):
    in_specs = (
        P("ckpt", ("groups", "ex"), "dim"),
        P("ckpt", ("groups", "ex"), "dim"),
        P("ckpt", ("groups", "ex")),
    )
    out_specs = P(("ckpt", "dim"), ("groups", "ex"))
    return jax.shard_map(local, mesh=mesh, in_specs=in_specs, out_specs=out_specs, check_vma=False)
```

```python
import jax
import jax.numpy as jnp
from jax import lax
from jax.sharding import PartitionSpec as P

PLACE = ("ex", "ckpt", "dim")


def after(value, *others):
    return lax.optimization_barrier((value,) + others)[0]


def weighted(checks, train, weights, scale):
    total = None
    for piece, examples, weight in zip(checks, train, weights):
        dots = lax.dot_general(
            piece,
            examples,
            (((1,), (1,)), ((), ())),
            preferred_element_type=jnp.float32,
        )
        term = dots * weight[None, :]
        total = term if total is None else total + term
    return total * scale


class Keepers:
    def __init__(self, rows):
        self.ckpts, self.dims = lax.axis_size("ckpt"), lax.axis_size("dim")
        self.planes = lax.axis_size("ex")
        self.z, self.x, self.c = [lax.axis_index(name) for name in PLACE]
        kept = rows * self.planes // (self.ckpts * self.dims)
        self.ratio = kept // rows
        assert self.ratio * rows == kept

    def index(self, z, x, c):
        return (z * self.ckpts + x) * self.dims + c

    def of(self, block):
        owner = block // self.ratio
        return owner // self.dims, owner % self.dims

    def mine(self, blocks, j=0):
        found = jnp.bool_(False)
        for z, block in enumerate(blocks):
            if block is not None and block % self.ratio == j:
                x, c = self.of(block)
                found = found | ((self.z == z) & (self.x == x) & (self.c == c))
        return found

    def near_sums(self, partial, blocks):
        total = partial
        for away in range(1, self.dims):
            pairs = []
            for z, block in enumerate(blocks):
                c = self.of(block)[1]
                for x in range(self.ckpts):
                    pairs.append((self.index(z, x, (c + away) % self.dims), self.index(z, x, c)))
            total = total + lax.ppermute(partial, PLACE, pairs)
        return total

    def far_sums(self, total, blocks):
        whole = total
        for away in range(1, self.ckpts):
            pairs = []
            for z, block in enumerate(blocks):
                x, c = self.of(block)
                pairs.append((self.index(z, (x + away) % self.ckpts, c), self.index(z, x, c)))
            whole = whole + lax.ppermute(total, PLACE, pairs)
        return whole


def ring(train_features, query_features, residual_weights, keepers, scale):
    planes, ratio = keepers.planes, keepers.ratio
    rows = query_features.shape[1]
    cut = rows // 2
    right = [(s, (s + 1) % planes) for s in range(planes)]
    left = [(s, (s - 1) % planes) for s in range(planes)]
    parts = []

    def finish(queries, step, *earlier):
        blocks = [(s + step) % planes for s in range(planes)]
        found = weighted(list(queries), train_features, residual_weights, scale)
        whole = keepers.far_sums(after(keepers.near_sums(found, blocks), *earlier), blocks)
        parts.append((blocks, whole))
        return whole

    def chosen(parts):
        found = []
        for j in range(ratio):
            kept = None
            for blocks, whole in parts:
                kept = whole if kept is None else jnp.where(keepers.mine(blocks, j), whole, kept)
            found.append(kept)
        return found

    from_left = from_right = query_features
    for step in range(1, planes // 2):
        from_right = lax.ppermute(from_right, "ex", left)
        from_left = lax.ppermute(from_left, "ex", right)
        if step == 1:
            own = finish(query_features, 0)
        ahead = finish(from_right, step)
        if step < planes // 2 - 1:
            finish(from_left, -step)
    low = lax.ppermute(from_right[:, cut:], "ex", left)
    top = lax.ppermute(after(from_left[:, :cut], low, own), "ex", right)
    behind = finish(after(from_left, low), -(planes // 2 - 1))
    earlier = list(parts)
    below = finish(low, planes // 2)
    above = finish(top, planes // 2, ahead, behind, below)
    across = parts[-1][0]
    tops = chosen([(blocks, whole[:cut]) for blocks, whole in earlier] + [(across, above)])
    lows = chosen([(blocks, whole[cut:]) for blocks, whole in earlier] + [(across, below)])
    return jnp.concatenate([part for both in zip(tops, lows) for part in both], axis=0)


def local(train_features, query_features, residual_weights):
    keepers = Keepers(query_features.shape[1])
    scale = 1.0 / (train_features.shape[0] * keepers.ckpts)
    return ring(train_features, query_features, residual_weights, keepers, scale)


def solution(mesh):
    in_specs = (
        P("ckpt", ("groups", "ex"), "dim"),
        P("ckpt", ("groups", "ex"), "dim"),
        P("ckpt", ("groups", "ex")),
    )
    out_specs = P(("ckpt", "dim"), ("groups", "ex"))
    return jax.shard_map(local, mesh=mesh, in_specs=in_specs, out_specs=out_specs, check_vma=False)
```

```python
import jax
import jax.numpy as jnp
from jax import lax
from jax.sharding import PartitionSpec as P

PLACE = ("ex", "ckpt", "dim")


def after(value, *others):
    return lax.optimization_barrier((value,) + others)[0]


def weighted(checks, train, weights, scale):
    total = None
    for piece, examples, weight in zip(checks, train, weights):
        dots = lax.dot_general(
            piece,
            examples,
            (((1,), (1,)), ((), ())),
            preferred_element_type=jnp.float32,
        )
        term = dots * weight[None, :]
        total = term if total is None else total + term
    return total * scale


class Keepers:
    def __init__(self, rows):
        self.ckpts, self.dims = lax.axis_size("ckpt"), lax.axis_size("dim")
        self.planes = lax.axis_size("ex")
        self.z, self.x, self.c = [lax.axis_index(name) for name in PLACE]
        kept = rows * self.planes // (self.ckpts * self.dims)
        self.ratio = kept // rows
        assert self.ratio * rows == kept

    def index(self, z, x, c):
        return (z * self.ckpts + x) * self.dims + c

    def of(self, block):
        owner = block // self.ratio
        return owner // self.dims, owner % self.dims

    def mine(self, blocks, j=0):
        found = jnp.bool_(False)
        for z, block in enumerate(blocks):
            if block is not None and block % self.ratio == j:
                x, c = self.of(block)
                found = found | ((self.z == z) & (self.x == x) & (self.c == c))
        return found

    def near_sums(self, partial, blocks):
        total = partial
        for away in range(1, self.dims):
            pairs = []
            for z, block in enumerate(blocks):
                c = self.of(block)[1]
                for x in range(self.ckpts):
                    pairs.append((self.index(z, x, (c + away) % self.dims), self.index(z, x, c)))
            total = total + lax.ppermute(partial, PLACE, pairs)
        return total

    def far_sums(self, total, blocks):
        whole = total
        for away in range(1, self.ckpts):
            pairs = []
            for z, block in enumerate(blocks):
                x, c = self.of(block)
                pairs.append((self.index(z, (x + away) % self.ckpts, c), self.index(z, x, c)))
            whole = whole + lax.ppermute(total, PLACE, pairs)
        return whole


def ring(train_features, query_features, residual_weights, keepers, scale):
    planes, ratio = keepers.planes, keepers.ratio
    rows = query_features.shape[1]
    cut = 3 * rows // 8
    right = [(s, (s + 1) % planes) for s in range(planes)]
    left = [(s, (s - 1) % planes) for s in range(planes)]
    parts = []

    def finish(queries, step, *earlier):
        blocks = [(s + step) % planes for s in range(planes)]
        found = weighted(list(queries), train_features, residual_weights, scale)
        whole = keepers.far_sums(keepers.near_sums(after(found, *earlier), blocks), blocks)
        parts.append((blocks, whole))
        return whole

    def chosen(parts):
        found = []
        for j in range(ratio):
            kept = None
            for blocks, whole in parts:
                kept = whole if kept is None else jnp.where(keepers.mine(blocks, j), whole, kept)
            found.append(kept)
        return found

    from_left = from_right = query_features
    for step in range(1, planes // 2):
        from_right = lax.ppermute(from_right, "ex", left)
        from_left = lax.ppermute(from_left, "ex", right)
        if step == 1:
            own = finish(query_features, 0)
        ahead = finish(from_right, step)
        if step < planes // 2 - 1:
            finish(from_left, -step)
    low = lax.ppermute(from_right[:, cut:], "ex", left)
    top = lax.ppermute(after(from_left[:, :cut], low, own), "ex", right)
    behind = finish(from_left, -(planes // 2 - 1), low, ahead)
    earlier = list(parts)
    below = finish(low, planes // 2)
    above = finish(after(top, behind), planes // 2, below)
    across = parts[-1][0]
    tops = chosen([(blocks, whole[:cut]) for blocks, whole in earlier] + [(across, above)])
    lows = chosen([(blocks, whole[cut:]) for blocks, whole in earlier] + [(across, below)])
    return jnp.concatenate([part for both in zip(tops, lows) for part in both], axis=0)


def local(train_features, query_features, residual_weights):
    keepers = Keepers(query_features.shape[1])
    scale = 1.0 / (train_features.shape[0] * keepers.ckpts)
    return ring(train_features, query_features, residual_weights, keepers, scale)


def solution(mesh):
    in_specs = (
        P("ckpt", ("groups", "ex"), "dim"),
        P("ckpt", ("groups", "ex"), "dim"),
        P("ckpt", ("groups", "ex")),
    )
    out_specs = P(("ckpt", "dim"), ("groups", "ex"))
    return jax.shard_map(local, mesh=mesh, in_specs=in_specs, out_specs=out_specs, check_vma=False)
```

```python
import jax
import jax.numpy as jnp
from jax import lax
from jax.sharding import PartitionSpec as P

PLACE = ("ex", "ckpt", "dim")


def after(value, *others):
    return lax.optimization_barrier((value,) + others)[0]


def weighted(checks, train, weights, scale):
    total = None
    for piece, examples, weight in zip(checks, train, weights):
        dots = lax.dot_general(
            piece,
            examples,
            (((1,), (1,)), ((), ())),
            preferred_element_type=jnp.float32,
        )
        term = dots * weight[None, :]
        total = term if total is None else total + term
    return total * scale


class Keepers:
    def __init__(self, rows):
        self.ckpts, self.dims = lax.axis_size("ckpt"), lax.axis_size("dim")
        self.planes = lax.axis_size("ex")
        self.z, self.x, self.c = [lax.axis_index(name) for name in PLACE]
        kept = rows * self.planes // (self.ckpts * self.dims)
        self.ratio = kept // rows
        assert self.ratio * rows == kept

    def index(self, z, x, c):
        return (z * self.ckpts + x) * self.dims + c

    def of(self, block):
        owner = block // self.ratio
        return owner // self.dims, owner % self.dims

    def mine(self, blocks, j=0):
        found = jnp.bool_(False)
        for z, block in enumerate(blocks):
            if block is not None and block % self.ratio == j:
                x, c = self.of(block)
                found = found | ((self.z == z) & (self.x == x) & (self.c == c))
        return found

    def near_sums(self, partial, blocks):
        total = partial
        for away in range(1, self.dims):
            pairs = []
            for z, block in enumerate(blocks):
                c = self.of(block)[1]
                for x in range(self.ckpts):
                    pairs.append((self.index(z, x, (c + away) % self.dims), self.index(z, x, c)))
            total = total + lax.ppermute(partial, PLACE, pairs)
        return total

    def far_sums(self, total, blocks):
        whole = total
        for away in range(1, self.ckpts):
            pairs = []
            for z, block in enumerate(blocks):
                x, c = self.of(block)
                pairs.append((self.index(z, (x + away) % self.ckpts, c), self.index(z, x, c)))
            whole = whole + lax.ppermute(total, PLACE, pairs)
        return whole


def ring(train_features, query_features, residual_weights, keepers, scale):
    planes, ratio = keepers.planes, keepers.ratio
    rows = query_features.shape[1]
    cut = rows // 4
    right = [(s, (s + 1) % planes) for s in range(planes)]
    left = [(s, (s - 1) % planes) for s in range(planes)]
    parts = []

    def finish(queries, step, *earlier):
        blocks = [(s + step) % planes for s in range(planes)]
        found = weighted(list(queries), train_features, residual_weights, scale)
        whole = keepers.far_sums(keepers.near_sums(after(found, *earlier), blocks), blocks)
        parts.append((blocks, whole))
        return whole

    def chosen(parts):
        found = []
        for j in range(ratio):
            kept = None
            for blocks, whole in parts:
                kept = whole if kept is None else jnp.where(keepers.mine(blocks, j), whole, kept)
            found.append(kept)
        return found

    from_left = from_right = query_features
    for step in range(1, planes // 2):
        from_right = lax.ppermute(from_right, "ex", left)
        from_left = lax.ppermute(from_left, "ex", right)
        if step == 1:
            own = finish(query_features, 0)
        ahead = finish(from_right, step)
        if step < planes // 2 - 1:
            finish(from_left, -step)
    low = lax.ppermute(from_right[:, cut:], "ex", left)
    top = lax.ppermute(after(from_left[:, :cut], low, own), "ex", right)
    behind = finish(from_left, -(planes // 2 - 1), low, ahead)
    earlier = list(parts)
    below = finish(low, planes // 2)
    above = finish(after(top, behind), planes // 2, below)
    across = parts[-1][0]
    tops = chosen([(blocks, whole[:cut]) for blocks, whole in earlier] + [(across, above)])
    lows = chosen([(blocks, whole[cut:]) for blocks, whole in earlier] + [(across, below)])
    return jnp.concatenate([part for both in zip(tops, lows) for part in both], axis=0)


def local(train_features, query_features, residual_weights):
    keepers = Keepers(query_features.shape[1])
    scale = 1.0 / (train_features.shape[0] * keepers.ckpts)
    return ring(train_features, query_features, residual_weights, keepers, scale)


def solution(mesh):
    in_specs = (
        P("ckpt", ("groups", "ex"), "dim"),
        P("ckpt", ("groups", "ex"), "dim"),
        P("ckpt", ("groups", "ex")),
    )
    out_specs = P(("ckpt", "dim"), ("groups", "ex"))
    return jax.shard_map(local, mesh=mesh, in_specs=in_specs, out_specs=out_specs, check_vma=False)
```

```python
import jax
import jax.numpy as jnp
from jax import lax
from jax.sharding import PartitionSpec as P

PLACE = ("ex", "ckpt", "dim")


def after(value, *others):
    return lax.optimization_barrier((value,) + others)[0]


def weighted(checks, train, weights, scale):
    total = None
    for piece, examples, weight in zip(checks, train, weights):
        dots = lax.dot_general(
            piece,
            examples,
            (((1,), (1,)), ((), ())),
            preferred_element_type=jnp.float32,
        )
        term = dots * weight[None, :]
        total = term if total is None else total + term
    return total * scale


class Keepers:
    def __init__(self, rows):
        self.ckpts, self.dims = lax.axis_size("ckpt"), lax.axis_size("dim")
        self.planes = lax.axis_size("ex")
        self.z, self.x, self.c = [lax.axis_index(name) for name in PLACE]
        kept = rows * self.planes // (self.ckpts * self.dims)
        self.ratio = kept // rows
        assert self.ratio * rows == kept

    def index(self, z, x, c):
        return (z * self.ckpts + x) * self.dims + c

    def of(self, block):
        owner = block // self.ratio
        return owner // self.dims, owner % self.dims

    def mine(self, blocks, j=0):
        found = jnp.bool_(False)
        for z, block in enumerate(blocks):
            if block is not None and block % self.ratio == j:
                x, c = self.of(block)
                found = found | ((self.z == z) & (self.x == x) & (self.c == c))
        return found

    def near_sums(self, partial, blocks):
        total = partial
        for away in range(1, self.dims):
            pairs = []
            for z, block in enumerate(blocks):
                c = self.of(block)[1]
                for x in range(self.ckpts):
                    pairs.append((self.index(z, x, (c + away) % self.dims), self.index(z, x, c)))
            total = total + lax.ppermute(partial, PLACE, pairs)
        return total

    def far_sums(self, total, blocks):
        whole = total
        for away in range(1, self.ckpts):
            pairs = []
            for z, block in enumerate(blocks):
                x, c = self.of(block)
                pairs.append((self.index(z, (x + away) % self.ckpts, c), self.index(z, x, c)))
            whole = whole + lax.ppermute(total, PLACE, pairs)
        return whole


def ring(train_features, query_features, residual_weights, keepers, scale):
    planes, ratio = keepers.planes, keepers.ratio
    rows = query_features.shape[1]
    cut = 3 * rows // 8
    right = [(s, (s + 1) % planes) for s in range(planes)]
    left = [(s, (s - 1) % planes) for s in range(planes)]
    tops, lows = [], []

    def finish(queries, step, into, near=(), far=()):
        blocks = [(s + step) % planes for s in range(planes)]
        found = weighted(list(queries), train_features, residual_weights, scale)
        total = keepers.near_sums(after(found, *near) if near else found, blocks)
        whole = keepers.far_sums(after(total, *far) if far else total, blocks)
        for parts in into:
            part = whole
            if len(into) == 2:
                part = whole[:cut] if parts is tops else whole[cut:]
            parts.append((blocks, part))
        return whole

    def chosen(parts):
        found = []
        for j in range(ratio):
            kept = None
            for blocks, part in parts:
                kept = part if kept is None else jnp.where(keepers.mine(blocks, j), part, kept)
            found.append(kept)
        return found

    both = (tops, lows)
    half = planes // 2
    from_left = from_right = query_features
    for step in range(1, half - 1):
        from_right = lax.ppermute(from_right, "ex", left)
        from_left = lax.ppermute(from_left, "ex", right)
        finish(from_right, step, both)
        finish(from_left, -step, both)
    own = finish(query_features, 0, both)
    from_right = lax.ppermute(from_right, "ex", left)
    from_left = lax.ppermute(from_left, "ex", right)
    low = lax.ppermute(from_right[:, cut:], "ex", left)
    top = lax.ppermute(after(from_right[:, :cut], low), "ex", left)
    ahead = finish(from_right, half - 1, both)
    behind = finish(from_left, 1 - half, both, far=(low, own, ahead))
    below = finish(low, half, (lows,))
    finish(top, half, (tops,), near=(behind,), far=(below,))
    return jnp.concatenate([part for pair in zip(chosen(tops), chosen(lows)) for part in pair], axis=0)


def local(train_features, query_features, residual_weights):
    keepers = Keepers(query_features.shape[1])
    scale = 1.0 / (train_features.shape[0] * keepers.ckpts)
    return ring(train_features, query_features, residual_weights, keepers, scale)


def solution(mesh):
    in_specs = (
        P("ckpt", ("groups", "ex"), "dim"),
        P("ckpt", ("groups", "ex"), "dim"),
        P("ckpt", ("groups", "ex")),
    )
    out_specs = P(("ckpt", "dim"), ("groups", "ex"))
    return jax.shard_map(local, mesh=mesh, in_specs=in_specs, out_specs=out_specs, check_vma=False)
```

```python
import jax
import jax.numpy as jnp
from jax import lax
from jax.sharding import PartitionSpec as P

PLACE = ("ex", "ckpt", "dim")


def after(value, *others):
    return lax.optimization_barrier((value,) + others)[0]


def weighted(checks, train, weights, scale):
    total = None
    for piece, examples, weight in zip(checks, train, weights):
        dots = lax.dot_general(
            piece,
            examples,
            (((1,), (1,)), ((), ())),
            preferred_element_type=jnp.float32,
        )
        term = dots * weight[None, :]
        total = term if total is None else total + term
    return total * scale


class Keepers:
    def __init__(self, rows):
        self.ckpts, self.dims = lax.axis_size("ckpt"), lax.axis_size("dim")
        self.planes = lax.axis_size("ex")
        self.z, self.x, self.c = [lax.axis_index(name) for name in PLACE]
        kept = rows * self.planes // (self.ckpts * self.dims)
        self.ratio = kept // rows
        assert self.ratio * rows == kept

    def index(self, z, x, c):
        return (z * self.ckpts + x) * self.dims + c

    def of(self, block):
        owner = block // self.ratio
        return owner // self.dims, owner % self.dims

    def mine(self, blocks, j=0):
        found = jnp.bool_(False)
        for z, block in enumerate(blocks):
            if block is not None and block % self.ratio == j:
                x, c = self.of(block)
                found = found | ((self.z == z) & (self.x == x) & (self.c == c))
        return found

    def near_sums(self, partial, blocks):
        total = partial
        for away in range(1, self.dims):
            pairs = []
            for z, block in enumerate(blocks):
                c = self.of(block)[1]
                for x in range(self.ckpts):
                    pairs.append((self.index(z, x, (c + away) % self.dims), self.index(z, x, c)))
            total = total + lax.ppermute(partial, PLACE, pairs)
        return total

    def far_sums(self, total, blocks):
        whole = total
        for away in range(1, self.ckpts):
            pairs = []
            for z, block in enumerate(blocks):
                x, c = self.of(block)
                pairs.append((self.index(z, (x + away) % self.ckpts, c), self.index(z, x, c)))
            whole = whole + lax.ppermute(total, PLACE, pairs)
        return whole


def ring(train_features, query_features, residual_weights, keepers, scale):
    planes, ratio = keepers.planes, keepers.ratio
    rows = query_features.shape[1]
    cut = 3 * rows // 8
    right = [(s, (s + 1) % planes) for s in range(planes)]
    left = [(s, (s - 1) % planes) for s in range(planes)]
    tops, lows = [], []

    def near(queries, step, *earlier):
        found = weighted(list(queries), train_features, residual_weights, scale)
        return keepers.near_sums(after(found, *earlier) if earlier else found, blocks_at(step))

    def far(total, step, into, *earlier):
        whole = keepers.far_sums(after(total, *earlier) if earlier else total, blocks_at(step))
        for parts in into:
            part = whole
            if len(into) == 2:
                part = whole[:cut] if parts is tops else whole[cut:]
            parts.append((blocks_at(step), part))
        return whole

    def blocks_at(step):
        return [(s + step) % planes for s in range(planes)]

    def chosen(parts):
        found = []
        for j in range(ratio):
            kept = None
            for blocks, part in parts:
                kept = part if kept is None else jnp.where(keepers.mine(blocks, j), part, kept)
            found.append(kept)
        return found

    both = (tops, lows)
    half = planes // 2
    from_left = from_right = query_features
    for step in range(1, half - 1):
        from_right = lax.ppermute(from_right, "ex", left)
        from_left = lax.ppermute(from_left, "ex", right)
        far(near(from_right, step), step, both)
        far(near(from_left, -step), -step, both)
    own = far(near(query_features, 0), 0, both)
    step = half - 1
    from_right = lax.ppermute(from_right, "ex", left)
    from_left = lax.ppermute(from_left, "ex", right)
    low = lax.ppermute(from_right[:, cut:], "ex", left)
    top = lax.ppermute(after(from_right[:, :cut], low), "ex", left)
    ahead = far(near(from_right, step), step, both)
    total = near(from_left, -step)
    behind = far(total, -step, both, low, own, ahead)
    below = far(near(low, half, behind), half, (lows,))
    far(near(top, half), half, (tops,), below)
    return jnp.concatenate([part for pair in zip(chosen(tops), chosen(lows)) for part in pair], axis=0)


def local(train_features, query_features, residual_weights):
    keepers = Keepers(query_features.shape[1])
    scale = 1.0 / (train_features.shape[0] * keepers.ckpts)
    return ring(train_features, query_features, residual_weights, keepers, scale)


def solution(mesh):
    in_specs = (
        P("ckpt", ("groups", "ex"), "dim"),
        P("ckpt", ("groups", "ex"), "dim"),
        P("ckpt", ("groups", "ex")),
    )
    out_specs = P(("ckpt", "dim"), ("groups", "ex"))
    return jax.shard_map(local, mesh=mesh, in_specs=in_specs, out_specs=out_specs, check_vma=False)
```

```python
import jax
import jax.numpy as jnp
from jax import lax
from jax.sharding import PartitionSpec as P

PLACE = ("ex", "ckpt", "dim")


def after(value, *others):
    return lax.optimization_barrier((value,) + others)[0]


def weighted(checks, train, weights, scale):
    total = None
    for piece, examples, weight in zip(checks, train, weights):
        dots = lax.dot_general(
            piece,
            examples,
            (((1,), (1,)), ((), ())),
            preferred_element_type=jnp.float32,
        )
        term = dots * weight[None, :]
        total = term if total is None else total + term
    return total * scale


class Keepers:
    def __init__(self, rows):
        self.ckpts, self.dims = lax.axis_size("ckpt"), lax.axis_size("dim")
        self.planes = lax.axis_size("ex")
        self.z, self.x, self.c = [lax.axis_index(name) for name in PLACE]
        kept = rows * self.planes // (self.ckpts * self.dims)
        self.ratio = kept // rows
        assert self.ratio * rows == kept

    def index(self, z, x, c):
        return (z * self.ckpts + x) * self.dims + c

    def of(self, block):
        owner = block // self.ratio
        return owner // self.dims, owner % self.dims

    def mine(self, blocks, j=0):
        found = jnp.bool_(False)
        for z, block in enumerate(blocks):
            if block is not None and block % self.ratio == j:
                x, c = self.of(block)
                found = found | ((self.z == z) & (self.x == x) & (self.c == c))
        return found

    def near_sums(self, partial, blocks):
        total = partial
        for away in range(1, self.dims):
            pairs = []
            for z, block in enumerate(blocks):
                c = self.of(block)[1]
                for x in range(self.ckpts):
                    pairs.append((self.index(z, x, (c + away) % self.dims), self.index(z, x, c)))
            total = total + lax.ppermute(partial, PLACE, pairs)
        return total

    def far_sums(self, total, blocks):
        whole = total
        for away in range(1, self.ckpts):
            pairs = []
            for z, block in enumerate(blocks):
                x, c = self.of(block)
                pairs.append((self.index(z, (x + away) % self.ckpts, c), self.index(z, x, c)))
            whole = whole + lax.ppermute(total, PLACE, pairs)
        return whole


def ring(train_features, query_features, residual_weights, keepers, scale):
    planes, ratio = keepers.planes, keepers.ratio
    rows = query_features.shape[1]
    cut = 5 * rows // 8
    right = [(s, (s + 1) % planes) for s in range(planes)]
    left = [(s, (s - 1) % planes) for s in range(planes)]
    tops, lows = [], []

    def near(queries, step, *earlier):
        found = weighted(list(queries), train_features, residual_weights, scale)
        return keepers.near_sums(after(found, *earlier) if earlier else found, blocks_at(step))

    def far(total, step, into, *earlier):
        whole = keepers.far_sums(after(total, *earlier) if earlier else total, blocks_at(step))
        for parts in into:
            part = whole
            if len(into) == 2:
                part = whole[:cut] if parts is tops else whole[cut:]
            parts.append((blocks_at(step), part))
        return whole

    def blocks_at(step):
        return [(s + step) % planes for s in range(planes)]

    def chosen(parts):
        found = []
        for j in range(ratio):
            kept = None
            for blocks, part in parts:
                kept = part if kept is None else jnp.where(keepers.mine(blocks, j), part, kept)
            found.append(kept)
        return found

    both = (tops, lows)
    half = planes // 2
    from_left = from_right = query_features
    for step in range(1, half - 1):
        from_right = lax.ppermute(from_right, "ex", left)
        from_left = lax.ppermute(from_left, "ex", right)
        far(near(from_right, step), step, both)
        far(near(from_left, -step), -step, both)
    own = far(near(query_features, 0), 0, both)
    step = half - 1
    from_right = lax.ppermute(from_right, "ex", left)
    from_left = lax.ppermute(from_left, "ex", right)
    low = lax.ppermute(from_right[:, cut:], "ex", left)
    top = lax.ppermute(after(from_right[:, :cut], low), "ex", left)
    ahead = far(near(from_right, step), step, both)
    total = near(from_left, -step)
    behind = far(total, -step, both, low, own, ahead)
    below = far(near(low, half), half, (lows,))
    far(near(top, half, behind), half, (tops,), below)
    return jnp.concatenate([part for pair in zip(chosen(tops), chosen(lows)) for part in pair], axis=0)


def local(train_features, query_features, residual_weights):
    keepers = Keepers(query_features.shape[1])
    scale = 1.0 / (train_features.shape[0] * keepers.ckpts)
    return ring(train_features, query_features, residual_weights, keepers, scale)


def solution(mesh):
    in_specs = (
        P("ckpt", ("groups", "ex"), "dim"),
        P("ckpt", ("groups", "ex"), "dim"),
        P("ckpt", ("groups", "ex")),
    )
    out_specs = P(("ckpt", "dim"), ("groups", "ex"))
    return jax.shard_map(local, mesh=mesh, in_specs=in_specs, out_specs=out_specs, check_vma=False)
```

```python
import jax
import jax.numpy as jnp
from jax import lax
from jax.sharding import PartitionSpec as P

PLACE = ("ex", "ckpt", "dim")


def after(value, *others):
    return lax.optimization_barrier((value,) + others)[0]


def weighted(checks, train, weights, scale):
    total = None
    for piece, examples, weight in zip(checks, train, weights):
        dots = lax.dot_general(
            piece,
            examples,
            (((1,), (1,)), ((), ())),
            preferred_element_type=jnp.float32,
        )
        term = dots * weight[None, :]
        total = term if total is None else total + term
    return total * scale


class Keepers:
    def __init__(self, rows):
        self.ckpts, self.dims = lax.axis_size("ckpt"), lax.axis_size("dim")
        self.planes = lax.axis_size("ex")
        self.z, self.x, self.c = [lax.axis_index(name) for name in PLACE]
        kept = rows * self.planes // (self.ckpts * self.dims)
        self.ratio = kept // rows
        assert self.ratio * rows == kept

    def index(self, z, x, c):
        return (z * self.ckpts + x) * self.dims + c

    def of(self, block):
        owner = block // self.ratio
        return owner // self.dims, owner % self.dims

    def mine(self, blocks, j=0):
        found = jnp.bool_(False)
        for z, block in enumerate(blocks):
            if block is not None and block % self.ratio == j:
                x, c = self.of(block)
                found = found | ((self.z == z) & (self.x == x) & (self.c == c))
        return found

    def near_sums(self, partial, blocks):
        total = partial
        for away in range(1, self.dims):
            pairs = []
            for z, block in enumerate(blocks):
                c = self.of(block)[1]
                for x in range(self.ckpts):
                    pairs.append((self.index(z, x, (c + away) % self.dims), self.index(z, x, c)))
            total = total + lax.ppermute(partial, PLACE, pairs)
        return total

    def far_sums(self, total, blocks):
        whole = total
        for away in range(1, self.ckpts):
            pairs = []
            for z, block in enumerate(blocks):
                x, c = self.of(block)
                pairs.append((self.index(z, (x + away) % self.ckpts, c), self.index(z, x, c)))
            whole = whole + lax.ppermute(total, PLACE, pairs)
        return whole


def ring(train_features, query_features, residual_weights, keepers, scale):
    planes, ratio = keepers.planes, keepers.ratio
    rows = query_features.shape[1]
    cut = rows // 2
    right = [(s, (s + 1) % planes) for s in range(planes)]
    left = [(s, (s - 1) % planes) for s in range(planes)]
    tops, lows = [], []

    def near(queries, step, *earlier):
        found = weighted(list(queries), train_features, residual_weights, scale)
        return keepers.near_sums(after(found, *earlier) if earlier else found, blocks_at(step))

    def far(total, step, into, *earlier):
        whole = keepers.far_sums(after(total, *earlier) if earlier else total, blocks_at(step))
        for parts in into:
            part = whole
            if len(into) == 2:
                part = whole[:cut] if parts is tops else whole[cut:]
            parts.append((blocks_at(step), part))
        return whole

    def blocks_at(step):
        return [(s + step) % planes for s in range(planes)]

    def chosen(parts):
        found = []
        for j in range(ratio):
            kept = None
            for blocks, part in parts:
                kept = part if kept is None else jnp.where(keepers.mine(blocks, j), part, kept)
            found.append(kept)
        return found

    both = (tops, lows)
    half = planes // 2
    from_left = from_right = query_features
    for step in range(1, half - 1):
        from_right = lax.ppermute(from_right, "ex", left)
        from_left = lax.ppermute(from_left, "ex", right)
        far(near(from_right, step), step, both)
        far(near(from_left, -step), -step, both)
    own = far(near(query_features, 0), 0, both)
    step = half - 1
    from_right = lax.ppermute(from_right, "ex", left)
    from_left = lax.ppermute(from_left, "ex", right)
    low = lax.ppermute(from_right[:, cut:], "ex", left)
    top = lax.ppermute(from_right[:, :cut], "ex", left)
    ahead = far(near(from_right, step), step, both)
    total = near(from_left, -step)
    behind = far(total, -step, both, low, own, ahead)
    below = far(near(low, half), half, (lows,))
    far(near(top, half, behind), half, (tops,), below)
    return jnp.concatenate([part for pair in zip(chosen(tops), chosen(lows)) for part in pair], axis=0)


def local(train_features, query_features, residual_weights):
    keepers = Keepers(query_features.shape[1])
    scale = 1.0 / (train_features.shape[0] * keepers.ckpts)
    return ring(train_features, query_features, residual_weights, keepers, scale)


def solution(mesh):
    in_specs = (
        P("ckpt", ("groups", "ex"), "dim"),
        P("ckpt", ("groups", "ex"), "dim"),
        P("ckpt", ("groups", "ex")),
    )
    out_specs = P(("ckpt", "dim"), ("groups", "ex"))
    return jax.shard_map(local, mesh=mesh, in_specs=in_specs, out_specs=out_specs, check_vma=False)
```

```python
import jax
import jax.numpy as jnp
from jax import lax
from jax.sharding import PartitionSpec as P

PLACE = ("ex", "ckpt", "dim")


def after(value, *others):
    return lax.optimization_barrier((value,) + others)[0]


def weighted(checks, train, weights, scale):
    total = None
    for piece, examples, weight in zip(checks, train, weights):
        dots = lax.dot_general(
            piece,
            examples,
            (((1,), (1,)), ((), ())),
            preferred_element_type=jnp.float32,
        )
        term = dots * weight[None, :]
        total = term if total is None else total + term
    return total * scale


class Keepers:
    def __init__(self, rows):
        self.ckpts, self.dims = lax.axis_size("ckpt"), lax.axis_size("dim")
        self.planes = lax.axis_size("ex")
        self.z, self.x, self.c = [lax.axis_index(name) for name in PLACE]
        kept = rows * self.planes // (self.ckpts * self.dims)
        self.ratio = kept // rows
        assert self.ratio * rows == kept

    def index(self, z, x, c):
        return (z * self.ckpts + x) * self.dims + c

    def of(self, block):
        owner = block // self.ratio
        return owner // self.dims, owner % self.dims

    def mine(self, blocks, j=0):
        found = jnp.bool_(False)
        for z, block in enumerate(blocks):
            if block is not None and block % self.ratio == j:
                x, c = self.of(block)
                found = found | ((self.z == z) & (self.x == x) & (self.c == c))
        return found

    def near_sums(self, partial, blocks):
        total = partial
        for away in range(1, self.dims):
            pairs = []
            for z, block in enumerate(blocks):
                c = self.of(block)[1]
                for x in range(self.ckpts):
                    pairs.append((self.index(z, x, (c + away) % self.dims), self.index(z, x, c)))
            total = total + lax.ppermute(partial, PLACE, pairs)
        return total

    def far_sums(self, total, blocks):
        whole = total
        for away in range(1, self.ckpts):
            pairs = []
            for z, block in enumerate(blocks):
                x, c = self.of(block)
                pairs.append((self.index(z, (x + away) % self.ckpts, c), self.index(z, x, c)))
            whole = whole + lax.ppermute(total, PLACE, pairs)
        return whole


def ring(train_features, query_features, residual_weights, keepers, scale):
    planes, ratio = keepers.planes, keepers.ratio
    rows = query_features.shape[1]
    cut = 5 * rows // 8
    right = [(s, (s + 1) % planes) for s in range(planes)]
    left = [(s, (s - 1) % planes) for s in range(planes)]
    tops, lows = [], []

    def near(queries, step, *earlier):
        found = weighted(list(queries), train_features, residual_weights, scale)
        return keepers.near_sums(after(found, *earlier) if earlier else found, blocks_at(step))

    def far(total, step, into, *earlier):
        whole = keepers.far_sums(after(total, *earlier) if earlier else total, blocks_at(step))
        for parts in into:
            part = whole
            if len(into) == 2:
                part = whole[:cut] if parts is tops else whole[cut:]
            parts.append((blocks_at(step), part))
        return whole

    def blocks_at(step):
        return [(s + step) % planes for s in range(planes)]

    def chosen(parts):
        found = []
        for j in range(ratio):
            kept = None
            for blocks, part in parts:
                kept = part if kept is None else jnp.where(keepers.mine(blocks, j), part, kept)
            found.append(kept)
        return found

    both = (tops, lows)
    half = planes // 2
    from_left = from_right = query_features
    for step in range(1, half - 1):
        from_right = lax.ppermute(from_right, "ex", left)
        from_left = lax.ppermute(from_left, "ex", right)
        far(near(from_right, step), step, both)
        far(near(from_left, -step), -step, both)
    own = far(near(query_features, 0), 0, both)
    step = half - 1
    from_right = lax.ppermute(from_right, "ex", left)
    from_left = lax.ppermute(from_left, "ex", right)
    low = lax.ppermute(from_right[:, cut:], "ex", left)
    ahead = far(near(from_right, step), step, both)
    top = lax.ppermute(after(from_right[:, :cut], ahead), "ex", left)
    total = near(from_left, -step)
    behind = far(total, -step, both, low, own, ahead)
    below = far(near(low, half), half, (lows,))
    far(near(top, half, behind), half, (tops,), below)
    return jnp.concatenate([part for pair in zip(chosen(tops), chosen(lows)) for part in pair], axis=0)


def local(train_features, query_features, residual_weights):
    keepers = Keepers(query_features.shape[1])
    scale = 1.0 / (train_features.shape[0] * keepers.ckpts)
    return ring(train_features, query_features, residual_weights, keepers, scale)


def solution(mesh):
    in_specs = (
        P("ckpt", ("groups", "ex"), "dim"),
        P("ckpt", ("groups", "ex"), "dim"),
        P("ckpt", ("groups", "ex")),
    )
    out_specs = P(("ckpt", "dim"), ("groups", "ex"))
    return jax.shard_map(local, mesh=mesh, in_specs=in_specs, out_specs=out_specs, check_vma=False)
```

```python
import jax
import jax.numpy as jnp
from jax import lax
from jax.sharding import PartitionSpec as P

PLACE = ("ex", "ckpt", "dim")


def after(value, *others):
    return lax.optimization_barrier((value,) + others)[0]


def weighted(checks, train, weights, scale):
    total = None
    for piece, examples, weight in zip(checks, train, weights):
        dots = lax.dot_general(
            piece,
            examples,
            (((1,), (1,)), ((), ())),
            preferred_element_type=jnp.float32,
        )
        term = dots * weight[None, :]
        total = term if total is None else total + term
    return total * scale


class Keepers:
    def __init__(self, rows):
        self.ckpts, self.dims = lax.axis_size("ckpt"), lax.axis_size("dim")
        self.planes = lax.axis_size("ex")
        self.z, self.x, self.c = [lax.axis_index(name) for name in PLACE]
        kept = rows * self.planes // (self.ckpts * self.dims)
        self.ratio = kept // rows
        assert self.ratio * rows == kept

    def index(self, z, x, c):
        return (z * self.ckpts + x) * self.dims + c

    def of(self, block):
        owner = block // self.ratio
        return owner // self.dims, owner % self.dims

    def mine(self, blocks, j=0):
        found = jnp.bool_(False)
        for z, block in enumerate(blocks):
            if block is not None and block % self.ratio == j:
                x, c = self.of(block)
                found = found | ((self.z == z) & (self.x == x) & (self.c == c))
        return found

    def near_sums(self, partial, blocks):
        total = partial
        for away in range(1, self.dims):
            pairs = []
            for z, block in enumerate(blocks):
                c = self.of(block)[1]
                for x in range(self.ckpts):
                    pairs.append((self.index(z, x, (c + away) % self.dims), self.index(z, x, c)))
            total = total + lax.ppermute(partial, PLACE, pairs)
        return total

    def far_sums(self, total, blocks):
        whole = total
        for away in range(1, self.ckpts):
            pairs = []
            for z, block in enumerate(blocks):
                x, c = self.of(block)
                pairs.append((self.index(z, (x + away) % self.ckpts, c), self.index(z, x, c)))
            whole = whole + lax.ppermute(total, PLACE, pairs)
        return whole


def ring(train_features, query_features, residual_weights, keepers, scale):
    planes, ratio = keepers.planes, keepers.ratio
    rows = query_features.shape[1]
    cut = 5 * rows // 8
    right = [(s, (s + 1) % planes) for s in range(planes)]
    left = [(s, (s - 1) % planes) for s in range(planes)]
    tops, lows = [], []

    def near(queries, step, *earlier):
        found = weighted(list(queries), train_features, residual_weights, scale)
        return keepers.near_sums(after(found, *earlier) if earlier else found, blocks_at(step))

    def far(total, step, into, *earlier):
        whole = keepers.far_sums(after(total, *earlier) if earlier else total, blocks_at(step))
        for parts in into:
            part = whole
            if len(into) == 2:
                part = whole[:cut] if parts is tops else whole[cut:]
            parts.append((blocks_at(step), part))
        return whole

    def blocks_at(step):
        return [(s + step) % planes for s in range(planes)]

    def chosen(parts):
        found = []
        for j in range(ratio):
            kept = None
            for blocks, part in parts:
                kept = part if kept is None else jnp.where(keepers.mine(blocks, j), part, kept)
            found.append(kept)
        return found

    both = (tops, lows)
    half = planes // 2
    from_left = from_right = query_features
    for step in range(1, half - 1):
        from_right = lax.ppermute(from_right, "ex", left)
        from_left = lax.ppermute(from_left, "ex", right)
        far(near(from_right, step), step, both)
        far(near(from_left, -step), -step, both)
    own = far(near(query_features, 0), 0, both)
    step = half - 1
    from_right = lax.ppermute(from_right, "ex", left)
    from_left = lax.ppermute(from_left, "ex", right)
    low = lax.ppermute(from_right[:, cut:], "ex", left)
    top = lax.ppermute(from_right[:, :cut], "ex", left)
    ahead = far(near(from_right, step), step, both)
    total = near(from_left, -step)
    behind = far(total, -step, both, low, own, ahead)
    below = far(near(low, half), half, (lows,))
    far(near(top, half, behind), half, (tops,), below)
    return jnp.concatenate([part for pair in zip(chosen(tops), chosen(lows)) for part in pair], axis=0)


def local(train_features, query_features, residual_weights):
    keepers = Keepers(query_features.shape[1])
    scale = 1.0 / (train_features.shape[0] * keepers.ckpts)
    return ring(train_features, query_features, residual_weights, keepers, scale)


def solution(mesh):
    in_specs = (
        P("ckpt", ("groups", "ex"), "dim"),
        P("ckpt", ("groups", "ex"), "dim"),
        P("ckpt", ("groups", "ex")),
    )
    out_specs = P(("ckpt", "dim"), ("groups", "ex"))
    return jax.shard_map(local, mesh=mesh, in_specs=in_specs, out_specs=out_specs, check_vma=False)
```

```python
import jax
import jax.numpy as jnp
from jax import lax
from jax.sharding import PartitionSpec as P

PLACE = ("ex", "ckpt", "dim")


def after(value, *others):
    return lax.optimization_barrier((value,) + others)[0]


def weighted(checks, train, weights, scale):
    total = None
    for piece, examples, weight in zip(checks, train, weights):
        dots = lax.dot_general(
            piece,
            examples,
            (((1,), (1,)), ((), ())),
            preferred_element_type=jnp.float32,
        )
        term = dots * weight[None, :]
        total = term if total is None else total + term
    return total * scale


class Keepers:
    def __init__(self, rows):
        self.ckpts, self.dims = lax.axis_size("ckpt"), lax.axis_size("dim")
        self.planes = lax.axis_size("ex")
        self.z, self.x, self.c = [lax.axis_index(name) for name in PLACE]
        kept = rows * self.planes // (self.ckpts * self.dims)
        self.ratio = kept // rows
        assert self.ratio * rows == kept

    def index(self, z, x, c):
        return (z * self.ckpts + x) * self.dims + c

    def of(self, block):
        owner = block // self.ratio
        return owner // self.dims, owner % self.dims

    def mine(self, blocks, j=0):
        found = jnp.bool_(False)
        for z, block in enumerate(blocks):
            if block is not None and block % self.ratio == j:
                x, c = self.of(block)
                found = found | ((self.z == z) & (self.x == x) & (self.c == c))
        return found

    def near_sums(self, partial, blocks):
        total = partial
        for away in range(1, self.dims):
            pairs = []
            for z, block in enumerate(blocks):
                c = self.of(block)[1]
                for x in range(self.ckpts):
                    pairs.append((self.index(z, x, (c + away) % self.dims), self.index(z, x, c)))
            total = total + lax.ppermute(partial, PLACE, pairs)
        return total

    def far_sums(self, total, blocks):
        whole = total
        for away in range(1, self.ckpts):
            pairs = []
            for z, block in enumerate(blocks):
                x, c = self.of(block)
                pairs.append((self.index(z, (x + away) % self.ckpts, c), self.index(z, x, c)))
            whole = whole + lax.ppermute(total, PLACE, pairs)
        return whole


def ring(train_features, query_features, residual_weights, keepers, scale):
    planes, ratio = keepers.planes, keepers.ratio
    rows = query_features.shape[1]
    cut = 9 * rows // 16
    right = [(s, (s + 1) % planes) for s in range(planes)]
    left = [(s, (s - 1) % planes) for s in range(planes)]
    tops, lows = [], []

    def near(queries, step, *earlier):
        found = weighted(list(queries), train_features, residual_weights, scale)
        return keepers.near_sums(after(found, *earlier) if earlier else found, blocks_at(step))

    def far(total, step, into, *earlier):
        whole = keepers.far_sums(after(total, *earlier) if earlier else total, blocks_at(step))
        for parts in into:
            part = whole
            if len(into) == 2:
                part = whole[:cut] if parts is tops else whole[cut:]
            parts.append((blocks_at(step), part))
        return whole

    def blocks_at(step):
        return [(s + step) % planes for s in range(planes)]

    def chosen(parts):
        found = []
        for j in range(ratio):
            kept = None
            for blocks, part in parts:
                kept = part if kept is None else jnp.where(keepers.mine(blocks, j), part, kept)
            found.append(kept)
        return found

    both = (tops, lows)
    half = planes // 2
    from_left = from_right = query_features
    for step in range(1, half - 1):
        from_right = lax.ppermute(from_right, "ex", left)
        from_left = lax.ppermute(from_left, "ex", right)
        far(near(from_right, step), step, both)
        far(near(from_left, -step), -step, both)
    own = far(near(query_features, 0), 0, both)
    step = half - 1
    from_right = lax.ppermute(from_right, "ex", left)
    from_left = lax.ppermute(from_left, "ex", right)
    low = lax.ppermute(from_right[:, cut:], "ex", left)
    top = lax.ppermute(from_right[:, :cut], "ex", left)
    ahead = far(near(from_right, step), step, both)
    total = near(from_left, -step)
    behind = far(total, -step, both, low, own, ahead)
    below = far(near(low, half), half, (lows,))
    far(near(top, half, behind), half, (tops,), below)
    return jnp.concatenate([part for pair in zip(chosen(tops), chosen(lows)) for part in pair], axis=0)


def local(train_features, query_features, residual_weights):
    keepers = Keepers(query_features.shape[1])
    scale = 1.0 / (train_features.shape[0] * keepers.ckpts)
    return ring(train_features, query_features, residual_weights, keepers, scale)


def solution(mesh):
    in_specs = (
        P("ckpt", ("groups", "ex"), "dim"),
        P("ckpt", ("groups", "ex"), "dim"),
        P("ckpt", ("groups", "ex")),
    )
    out_specs = P(("ckpt", "dim"), ("groups", "ex"))
    return jax.shard_map(local, mesh=mesh, in_specs=in_specs, out_specs=out_specs, check_vma=False)
```

```python
import jax
import jax.numpy as jnp
from jax import lax
from jax.sharding import PartitionSpec as P

PLACE = ("ex", "ckpt", "dim")


def after(value, *others):
    return lax.optimization_barrier((value,) + others)[0]


def weighted(checks, train, weights, scale):
    total = None
    for piece, examples, weight in zip(checks, train, weights):
        dots = lax.dot_general(
            piece,
            examples,
            (((1,), (1,)), ((), ())),
            preferred_element_type=jnp.float32,
        )
        term = dots * weight[None, :]
        total = term if total is None else total + term
    return total * scale


class Keepers:
    def __init__(self, rows):
        self.ckpts, self.dims = lax.axis_size("ckpt"), lax.axis_size("dim")
        self.planes = lax.axis_size("ex")
        self.z, self.x, self.c = [lax.axis_index(name) for name in PLACE]
        kept = rows * self.planes // (self.ckpts * self.dims)
        self.ratio = kept // rows
        assert self.ratio * rows == kept

    def index(self, z, x, c):
        return (z * self.ckpts + x) * self.dims + c

    def of(self, block):
        owner = block // self.ratio
        return owner // self.dims, owner % self.dims

    def mine(self, blocks, j=0):
        found = jnp.bool_(False)
        for z, block in enumerate(blocks):
            if block is not None and block % self.ratio == j:
                x, c = self.of(block)
                found = found | ((self.z == z) & (self.x == x) & (self.c == c))
        return found

    def near_sums(self, partial, blocks):
        total = partial
        for away in range(1, self.dims):
            pairs = []
            for z, block in enumerate(blocks):
                c = self.of(block)[1]
                for x in range(self.ckpts):
                    pairs.append((self.index(z, x, (c + away) % self.dims), self.index(z, x, c)))
            total = total + lax.ppermute(partial, PLACE, pairs)
        return total

    def far_sums(self, total, blocks):
        whole = total
        for away in range(1, self.ckpts):
            pairs = []
            for z, block in enumerate(blocks):
                x, c = self.of(block)
                pairs.append((self.index(z, (x + away) % self.ckpts, c), self.index(z, x, c)))
            whole = whole + lax.ppermute(total, PLACE, pairs)
        return whole


def ring(train_features, query_features, residual_weights, keepers, scale):
    planes, ratio = keepers.planes, keepers.ratio
    rows = query_features.shape[1]
    cut = 5 * rows // 8
    right = [(s, (s + 1) % planes) for s in range(planes)]
    left = [(s, (s - 1) % planes) for s in range(planes)]
    tops, lows = [], []

    def near(queries, step, *earlier):
        found = weighted(list(queries), train_features, residual_weights, scale)
        return keepers.near_sums(after(found, *earlier) if earlier else found, blocks_at(step))

    def far(total, step, into, *earlier):
        whole = keepers.far_sums(after(total, *earlier) if earlier else total, blocks_at(step))
        for parts in into:
            part = whole
            if len(into) == 2:
                part = whole[:cut] if parts is tops else whole[cut:]
            parts.append((blocks_at(step), part))
        return whole

    def blocks_at(step):
        return [(s + step) % planes for s in range(planes)]

    def chosen(parts):
        found = []
        for j in range(ratio):
            kept = None
            for blocks, part in parts:
                kept = part if kept is None else jnp.where(keepers.mine(blocks, j), part, kept)
            found.append(kept)
        return found

    both = (tops, lows)
    half = planes // 2
    from_left = from_right = query_features
    for step in range(1, half - 1):
        from_right = lax.ppermute(from_right, "ex", left)
        from_left = lax.ppermute(from_left, "ex", right)
        far(near(from_right, step), step, both)
        far(near(from_left, -step), -step, both)
    own = far(near(query_features, 0), 0, both)
    step = half - 1
    from_right = lax.ppermute(from_right, "ex", left)
    from_left = lax.ppermute(from_left, "ex", right)
    low = lax.ppermute(from_right[:, cut:], "ex", left)
    total_ahead = near(from_right, step)
    ahead = far(total_ahead, step, both)
    top = lax.ppermute(after(from_right[:, :cut], total_ahead), "ex", left)
    total = near(from_left, -step)
    behind = far(total, -step, both, low, own, ahead)
    below = far(near(low, half), half, (lows,))
    far(near(top, half, behind), half, (tops,), below)
    return jnp.concatenate([part for pair in zip(chosen(tops), chosen(lows)) for part in pair], axis=0)


def local(train_features, query_features, residual_weights):
    keepers = Keepers(query_features.shape[1])
    scale = 1.0 / (train_features.shape[0] * keepers.ckpts)
    return ring(train_features, query_features, residual_weights, keepers, scale)


def solution(mesh):
    in_specs = (
        P("ckpt", ("groups", "ex"), "dim"),
        P("ckpt", ("groups", "ex"), "dim"),
        P("ckpt", ("groups", "ex")),
    )
    out_specs = P(("ckpt", "dim"), ("groups", "ex"))
    return jax.shard_map(local, mesh=mesh, in_specs=in_specs, out_specs=out_specs, check_vma=False)
```
